32 devices in a mesh: dp: 32 (over z, y, x, core).
Axes of the slice: x: 2, y: 2, z: 4, core: 2. Of those that a mesh axis runs over, the one named last changes fastest.
Arguments:
- hidden_in: bfloat16 [2048, 4096], P('dp'), may hold values from -6 to 6
- queries: bfloat16 [2048, 2048], P('dp'), may hold values from -16 to 16
- keys: bfloat16 [2048, 512], P('dp'), may hold values from -16 to 16
- values: bfloat16 [2048, 512], P('dp'), may hold values from -6 to 6
- grad_attn: bfloat16 [2048, 2048], P('dp'), may hold values from -6 to 6
- send_rows: int32 [4, 32], replicated, may hold values from -1 to 63, as said below
- slot_docs: int32 [32, 4], P('dp'), may hold values from -1 to 63, as said below
Outputs:
- grad_queries: bfloat16 [2048, 2048], P('dp')
- grad_keys: bfloat16 [2048, 512], P('dp')
- grad_values: bfloat16 [2048, 512], P('dp')
- grad_wv: float32 [4096, 512], P('dp')
The draws below stay inside these ranges and needn't reach their ends.
Inputs may be any that keep to these rules, and one draw needn't show every extreme that they name: `send_rows`: every owner sends the same local rows to a rank. Each local row appears exactly once. The rows sent to one rank form whole documents at consecutive slots, the local rows of a document consecutive and rising with the slot; a document has at most 4 local rows, and in every draw some rank has all 4 slots used. slot_docs[r, j] is -1 exactly where send_rows[j, r] is -1; slots with the same number hold one document, and distinct documents have distinct numbers.
All inputs are finite; a program needn't handle non-finite values.
Results may differ from the reference program's by a relative error of at most 0.0057.
Values may be sent and summed in bfloat16 or wider, within the bound.
A program may use at most 128 MiB of HBM per device.

```python
import math
import jax
import jax.numpy as jnp
from jax import lax

D = 4096
HQ = 16
HK = 4
DH = 128
MOST = 4
TOK_DEV = 64
TOKENS = 2048


def doc_layout(key):
    owners = TOKENS // TOK_DEV
    doc_lens = jax.random.randint(jax.random.fold_in(key, 11), (TOK_DEV,), 1, MOST + 1, dtype=jnp.int32)
    doc_lens = doc_lens.at[0].set(MOST)
    doc_ends = jnp.cumsum(doc_lens)
    doc_starts = doc_ends - doc_lens
    exists = doc_starts < TOK_DEV
    doc_lens = jnp.where(exists, jnp.minimum(doc_lens, TOK_DEV - doc_starts), 0).astype(jnp.int32)
    doc_cost = doc_lens * doc_lens
    doc_order = jnp.argsort(-doc_cost, stable=True).astype(jnp.int32)
    ranks = jnp.arange(owners, dtype=jnp.int32)

    def place_doc(state_pair, doc_index):
        rank_load, rank_used = state_pair
        doc_size = doc_lens[doc_index]
        can_fit = rank_used + doc_size <= MOST
        rank_score = jnp.where(can_fit, rank_load * owners + ranks, 2 ** 30)
        chosen = jnp.argmin(rank_score).astype(jnp.int32)
        first_slot = rank_used[chosen]
        to_grow = (ranks == chosen) & (doc_size > 0)
        rank_load = rank_load + jnp.where(to_grow, doc_size * doc_size, 0)
        rank_used = rank_used + jnp.where(to_grow, doc_size, 0)
        return ((rank_load, rank_used), (chosen, first_slot))
    start_pair = (jnp.zeros((owners,), jnp.int32), jnp.zeros((owners,), jnp.int32))
    unused, (chosen_ranks, first_slots) = lax.scan(place_doc, start_pair, doc_order)
    doc_dest = jnp.zeros((TOK_DEV,), jnp.int32).at[doc_order].set(chosen_ranks)
    doc_slot = jnp.zeros((TOK_DEV,), jnp.int32).at[doc_order].set(first_slots)
    start_marks = jnp.zeros((TOK_DEV,), jnp.int32).at[jnp.where(exists, doc_starts, TOK_DEV)].add(1, mode='drop')
    doc_of = jnp.cumsum(start_marks) - 1
    local_rows = jnp.arange(TOK_DEV, dtype=jnp.int32)
    rank_of = doc_dest[doc_of]
    slot_of = doc_slot[doc_of] + local_rows - doc_starts[doc_of]
    doc_number = (doc_starts + doc_lens - 1).astype(jnp.int32)[doc_of]
    send_list = jnp.full((MOST, owners), -1, jnp.int32).at[slot_of, rank_of].set(local_rows)
    doc_list = jnp.full((owners, MOST), -1, jnp.int32).at[rank_of, slot_of].set(doc_number.astype(jnp.int32))
    return (send_list, doc_list)


def draw_send_rows(key, part):
    return doc_layout(key)[0]


def draw_slot_docs(key, part):
    return doc_layout(key)[1]


def draw_queries(key, part):
    drawn = jax.random.truncated_normal(jax.random.fold_in(key, 81), -6.0, 6.0, (TOKENS, HQ * DH), jnp.float32)
    return drawn.astype(jnp.bfloat16)


def draw_keys(key, part):
    drawn = jax.random.truncated_normal(jax.random.fold_in(key, 91), -6.0, 6.0, (TOKENS, HK * DH), jnp.float32)
    return drawn.astype(jnp.bfloat16)


def with_spikes(values, stream_key, source, target, parts, factor):
    def block_of(axis_at):
        return (jnp.arange(values.shape[axis_at]) // (values.shape[axis_at] // parts)).reshape((-1,) + (1,) * (values.ndim - 1 - axis_at))

    first = jax.random.permutation(stream_key, parts)[block_of(target)]
    second = (block_of(target) + parts // 2) % parts
    return jnp.where((block_of(source) == first) | (block_of(source) == second), factor * values, values)


def steps_of(key, shape, pieces, smallest, high):
    factor_of = 1.0
    for axis_at, parts in pieces:
        heights = jax.random.uniform(jax.random.fold_in(jax.random.fold_in(key, 6), axis_at), (parts,), jnp.float32, smallest / len(pieces), high / len(pieces))
        factor_of = factor_of * jnp.repeat(jnp.exp(heights), shape[axis_at] // parts).reshape((-1,) + (1,) * (len(shape) - 1 - axis_at))
    return factor_of


def scatter_about(own_key, dims, scale, reach, split=(), held_as=jnp.bfloat16):
    level = steps_of(own_key, dims, split, -0.22, 0.18) if split else 1.0
    values = jax.random.normal(own_key, dims, jnp.float32) * scale * level
    return jnp.minimum(jnp.maximum(values, -reach), reach).astype(held_as)


def bell_draw_with(stream_key, extent, deviation, most, split, heavy, held_as=jnp.bfloat16):
    result = deviation * jax.random.normal(stream_key, extent, jnp.float32)
    if split:
        result = result * steps_of(stream_key, extent, split, -0.22, 0.18)
    return jnp.clip(with_spikes(result, jax.random.fold_in(stream_key, 3), *heavy), -most, most).astype(held_as)


def setup_inputs(seed: int = 0) -> dict:
    streams_of = jax.random.split(jax.random.key(seed), 8)
    return {
        "hidden_in": bell_draw_with(streams_of[0], (TOKENS, D), 1.0, 6.0, ((0, 32),), (0, 1, 32, 2.75)),
        "queries": draw_queries(jax.random.fold_in(streams_of[7], 71), 0),
        "keys": draw_keys(jax.random.fold_in(streams_of[7], 71), 0),
        "values": scatter_about(streams_of[3], (TOKENS, HK * DH), 1.0, 6.0, ((0, 32),)),
        "grad_attn": scatter_about(streams_of[4], (TOKENS, HQ * DH), 1.0, 6.0, ((0, 32),)),
        "send_rows": draw_send_rows(jax.random.fold_in(streams_of[7], 71), 0),
        "slot_docs": draw_slot_docs(jax.random.fold_in(streams_of[7], 71), 0),
    }


def attend_rows(q_rows, k_rows, v_rows, o_rows, segment):
    row_count = q_rows.shape[0]
    group_size = HQ // HK
    score_scale = 1.0 / math.sqrt(DH)
    order_ids = jnp.arange(row_count, dtype=jnp.int32)
    live_rows = segment >= 0
    allowed = (segment[:, None] == segment[None, :]) & (order_ids[None, :] <= order_ids[:, None]) & live_rows[:, None]
    q_four = q_rows.astype(jnp.float32).reshape(row_count, HK, group_size, DH)
    o_four = o_rows.astype(jnp.float32).reshape(row_count, HK, group_size, DH)
    k_three = k_rows.astype(jnp.float32).reshape(row_count, HK, DH)
    v_three = v_rows.astype(jnp.float32).reshape(row_count, HK, DH)
    grad_q_list = []
    grad_k_list = []
    grad_v_list = []
    for head_kv in range(HK):
        q_group = q_four[:, head_kv]
        o_group = o_four[:, head_kv]
        k_group = k_three[:, head_kv]
        v_group = v_three[:, head_kv]
        scores = jnp.einsum('qhd,kd->hqk', q_group, k_group) * score_scale
        scores = jnp.where(allowed[None], scores, jnp.float32(-1000000000.0))
        row_max = lax.optimization_barrier(jnp.max(scores, axis=-1, keepdims=True))
        weights = jnp.exp(scores - row_max)
        attn_probs = weights / lax.optimization_barrier(jnp.sum(weights, axis=-1, keepdims=True))
        attn_probs = jnp.where(live_rows[None, :, None], attn_probs, jnp.float32(0.0))
        probs_b = lax.optimization_barrier(attn_probs.astype(jnp.bfloat16)).astype(jnp.float32)
        grad_v_list.append(jnp.einsum('hqk,qhd->kd', probs_b, o_group))
        dprob = jnp.einsum('qhd,kd->hqk', o_group, v_group)
        row_delta = lax.optimization_barrier(jnp.sum(attn_probs * dprob, axis=-1, keepdims=True))
        dscore = lax.optimization_barrier((attn_probs * (dprob - row_delta) * score_scale).astype(jnp.bfloat16)).astype(jnp.float32)
        grad_q_list.append(jnp.einsum('hqk,kd->qhd', dscore, k_group))
        grad_k_list.append(jnp.einsum('hqk,qhd->kd', dscore, q_group))
    grad_q_rows = jnp.stack(grad_q_list, axis=1).reshape(row_count, HQ * DH).astype(jnp.bfloat16)
    grad_k_rows = jnp.stack(grad_k_list, axis=1).reshape(row_count, HK * DH).astype(jnp.bfloat16)
    grad_v_rows = jnp.stack(grad_v_list, axis=1).reshape(row_count, HK * DH).astype(jnp.bfloat16)
    return (grad_q_rows, grad_k_rows, grad_v_rows)

def reference(hidden_in, queries, keys, values, grad_attn, send_rows, slot_docs):
    owners = TOKENS // TOK_DEV

    def per_rank(outputs, rank):
        local_rows = send_rows[:, rank]
        live_slots = local_rows >= 0
        global_rows = (jnp.arange(owners, dtype=jnp.int32)[None, :] * TOK_DEV + jnp.maximum(local_rows, 0)[:, None]).reshape(-1).astype(jnp.int32)
        segment = jnp.broadcast_to(slot_docs[rank][:, None], (MOST, owners)).reshape(-1)
        results = attend_rows(queries[global_rows], keys[global_rows], values[global_rows], grad_attn[global_rows], segment)
        live_rows = jnp.broadcast_to(live_slots[:, None], (MOST, owners)).reshape(-1)
        targets = jnp.where(live_rows, global_rows, TOKENS).astype(jnp.int32)
        updated = tuple((whole.at[targets].set(part_rows, mode='drop') for whole, part_rows in zip(outputs, results)))
        return (updated, None)
    initial = (jnp.zeros((TOKENS, HQ * DH), jnp.bfloat16), jnp.zeros((TOKENS, HK * DH), jnp.bfloat16), jnp.zeros((TOKENS, HK * DH), jnp.bfloat16))
    outputs, unused = lax.scan(per_rank, initial, jnp.arange(owners, dtype=jnp.int32))
    grad_queries, grad_keys, grad_values = outputs
    grad_wv = jnp.dot(hidden_in.T, grad_values, preferred_element_type=jnp.float32) * (1.0 / math.sqrt(TOKENS))
    return (grad_queries, grad_keys, grad_values, grad_wv)
```

```python
import functools
import math

import jax
import jax.numpy as jnp
from jax import lax
from jax.experimental import pallas as pl
from jax.experimental.pallas import tpu as pltpu
from jax.sharding import PartitionSpec as P

HQ = 16
HK = 4
DH = 128
PER_KV = HQ // HK
ROWS = 8
HALO = 3
TEAM = 8
MESH = pl.DeviceIdType.MESH
F32 = jnp.float32
BF16 = jnp.bfloat16

Q_AT = 0
O_AT = PER_KV * ROWS
K_AT = 2 * PER_KV * ROWS
V_AT = K_AT + 2 * ROWS
IN_ROWS = V_AT + 2 * ROWS
BACK_ROWS = PER_KV * ROWS + 2 * ROWS


def dot(a, b, da, db):
    return lax.dot_general(a, b, (((da,), (db,)), ((), ())), preferred_element_type=F32)


def wait_bytes(ref, count, sem):
    view = ref.at[pl.ds(0, count)]
    pltpu.make_async_copy(view, view, sem).wait()


def kernel(
    n, width,
    hid_ref, q_ref, k_ref, v_ref, o_ref, rows_ref, docs_ref,
    dq_ref, dk_ref, dv_ref, dw_ref,
    q32, o32, k32, v32, stage, came, probs, acc_v, acc_k,
    back_v, home_v, back, home, hid_out, hid_in, gv, gv_in, part, term_out, term_in,
    sent, got,
):
    me = lax.axis_index("dp")
    tok = q_ref.shape[0]
    groups = n // HK
    teams = n // TEAM
    member = lax.rem(me, TEAM)
    team = lax.div(me, TEAM)
    group = lax.div(me, HK)
    scale = 1.0 / math.sqrt(DH)
    keys = n * 2 * ROWS
    chunk = 8
    q_rows = chunk * PER_KV * ROWS

    barrier = pltpu.get_barrier_semaphore()

    def greet(i, c):
        pl.semaphore_signal(
            barrier, inc=1, device_id=(lax.rem(me + i, n),), device_id_type=MESH
        )
        return c

    lax.fori_loop(1, n, greet, 0)

    q32[...] = q_ref[...].astype(F32)
    o32[...] = o_ref[...].astype(F32)
    k32[0:ROWS, :] = jnp.zeros((ROWS, k32.shape[1]), F32)
    v32[0:ROWS, :] = jnp.zeros((ROWS, v32.shape[1]), F32)
    k32[ROWS:, :] = k_ref[...].astype(F32)
    v32[ROWS:, :] = v_ref[...].astype(F32)
    lane = lax.broadcasted_iota(jnp.int32, (2 * ROWS, DH), 1)
    line = lax.broadcasted_iota(jnp.int32, (2 * ROWS, DH), 0)
    doc_line = jnp.zeros((2 * ROWS, DH), F32)
    for j in range(docs_ref.shape[1]):
        doc_line = jnp.where(lane == j, (docs_ref[0, j] + 1).astype(F32), doc_line)

    def pack(g, c):
        at = pl.multiple_of(g * ROWS, ROWS)
        for h in range(HK):
            parts = [
                table[pl.ds(at, ROWS), pl.ds((PER_KV * h + i) * DH, DH)]
                for table in (q32, o32)
                for i in range(PER_KV)
            ]
            k_part = k32[pl.ds(at, 2 * ROWS), pl.ds(h * DH, DH)]
            parts.append(jnp.where(line == 0, doc_line, k_part))
            parts.append(v32[pl.ds(at, 2 * ROWS), pl.ds(h * DH, DH)])
            stage[HK * g + h] = jnp.concatenate(parts, axis=0).astype(BF16)
        return c

    lax.fori_loop(0, groups, pack, 0)
    came[me] = stage[me]

    pl.semaphore_wait(barrier, n - 1)

    def to_all(src, dst, index):
        def send(i, c):
            peer = lax.rem(me + i, n)
            pltpu.make_async_remote_copy(
                src.at[peer], dst.at[me], sent.at[index], got.at[index],
                device_id=(peer,), device_id_type=MESH,
            ).start()
            return c

        lax.fori_loop(1, n, send, 0)

    def to_team(src_of, dst, index):
        for i in range(1, TEAM):
            other = lax.rem(member + i, TEAM)
            pltpu.make_async_remote_copy(
                src_of(other), dst.at[member], sent.at[index], got.at[index],
                device_id=(team * TEAM + other,), device_id_type=MESH,
            ).start()

    to_all(stage, came, 0)

    span = hid_out.shape[2]
    for m in range(TEAM):
        if width % DH == 0:
            for p in range(teams):
                hid_out[m, :, p * width : (p + 1) * width] = hid_ref[
                    :, (p * TEAM + m) * width : (p * TEAM + m + 1) * width
                ]
        else:
            hid_out[m] = hid_ref[:, m * span : (m + 1) * span]
    hid_in[member] = hid_out[member]
    to_team(lambda other: hid_out.at[other], hid_in, 1)

    acc_v[...] = jnp.zeros_like(acc_v)
    acc_k[...] = jnp.zeros_like(acc_k)
    home_v[n:, :, :] = jnp.zeros((HK, 2 * ROWS, DH), BF16)
    home[n:, :, :] = jnp.zeros((HK, BACK_ROWS, DH), BF16)

    wait_bytes(came, n - 1, got.at[0])

    doc_rows = came[:, K_AT : K_AT + 2 * ROWS, :].reshape(n, 2 * ROWS, DH)[:, 0, :]
    pick = (
        lax.broadcasted_iota(jnp.int32, (8, DH), 0) == lax.broadcasted_iota(jnp.int32, (8, DH), 1)
    ).astype(F32).astype(BF16)
    doc_table = dot(pick, doc_rows, 1, 1)
    loc = lax.broadcasted_iota(jnp.int32, (2 * ROWS, n), 0) + (group - 1) * ROWS
    doc_sum = jnp.zeros((2 * ROWS, n), F32)
    for j in range(rows_ref.shape[0]):
        doc_sum += jnp.where(rows_ref[j : j + 1, :] == loc, doc_table[j : j + 1, :], 0.0)
    docs = jnp.sum(doc_sum, axis=1, keepdims=True)
    own_docs = docs[ROWS:]
    back_count = jnp.zeros((ROWS, 1), F32)
    for d in range(1, HALO + 1):
        back_count += jnp.where(docs[ROWS - d : 2 * ROWS - d] == own_docs, 1.0, 0.0)
    first = (
        lax.broadcasted_iota(jnp.int32, (ROWS, 1), 0) - back_count.astype(jnp.int32)
    ) * n
    first = jnp.broadcast_to(first[None], (q_rows // ROWS, ROWS, 1)).reshape(q_rows, 1)
    col = lax.broadcasted_iota(jnp.int32, (1, keys), 1)
    k_pos = (lax.rem(col, 2 * ROWS) - ROWS) * n + lax.div(col, 2 * ROWS)
    row = lax.broadcasted_iota(jnp.int32, (q_rows, 1), 0)
    q_pos = lax.rem(row, ROWS) * n + lax.div(row, PER_KV * ROWS)

    def rows_of(c, at):
        return came[pl.ds(c * chunk, chunk), at : at + PER_KV * ROWS, :].reshape(q_rows, DH)

    def keys_of(at):
        return came[:, at : at + 2 * ROWS, :].reshape(keys, DH)

    def prob_of(c):
        scores = dot(rows_of(c, Q_AT), keys_of(K_AT), 1, 1) * scale
        allowed = (k_pos >= first) & (k_pos <= q_pos + c * chunk)
        scores = jnp.where(allowed, scores, -1000000000.0)
        weights = jnp.exp(scores - jnp.max(scores, axis=1, keepdims=True))
        return weights * (1.0 / jnp.sum(weights, axis=1, keepdims=True))

    def soft(c, carry):
        p = prob_of(c)
        if probs.shape[0] > q_rows:
            probs[pl.ds(pl.multiple_of(c * q_rows, q_rows), q_rows), :] = p
        acc_v[...] += dot(p.astype(BF16), rows_of(c, O_AT), 0, 0)
        return carry

    lax.fori_loop(0, n // chunk, soft, 0)
    back_v[...] = acc_v[...].reshape(n, 2 * ROWS, DH).astype(BF16)
    home_v[me] = back_v[me]
    to_all(back_v, home_v, 2)

    def grads(c, carry):
        if probs.shape[0] > q_rows:
            p = probs[pl.ds(pl.multiple_of(c * q_rows, q_rows), q_rows), :]
        else:
            p = prob_of(c)
        dprob = dot(rows_of(c, O_AT), keys_of(V_AT), 1, 1)
        delta = jnp.sum(p * dprob, axis=1, keepdims=True)
        dscore = (p * (dprob - delta) * scale).astype(BF16)
        dq = dot(dscore, keys_of(K_AT), 1, 0).astype(BF16)
        back[pl.ds(c * chunk, chunk), 0 : PER_KV * ROWS, :] = dq.reshape(chunk, PER_KV * ROWS, DH)
        acc_k[...] += dot(dscore, rows_of(c, Q_AT), 0, 0)
        return carry

    lax.fori_loop(0, n // chunk, grads, 0)
    back[:, PER_KV * ROWS :, :] = acc_k[...].reshape(n, 2 * ROWS, DH).astype(BF16)
    home[me] = back[me]
    to_all(back, home, 3)

    def summed(ref, g, h, at):
        own = ref[HK * g + h, at : at + 2 * ROWS, :].astype(F32)
        after = ref[HK * g + HK + h, at : at + 2 * ROWS, :].astype(F32)
        return own[ROWS:] + after[:ROWS]

    wait_bytes(home_v, n - 1, got.at[2])

    def place_v(pair, c):
        at = pl.multiple_of(pair * 2 * ROWS, 2 * ROWS)
        for h in range(HK):
            both = [summed(home_v, 2 * pair + s, h, 0) for s in range(2)]
            gv[pl.ds(at, 2 * ROWS), pl.ds(h * DH, DH)] = jnp.concatenate(both, axis=0).astype(BF16)
        return c

    lax.fori_loop(0, groups // 2, place_v, 0)
    to_team(lambda other: gv, gv_in, 4)
    gv_in[member] = gv[...]
    dv_ref[...] = gv[...]
    wait_bytes(hid_in, TEAM - 1, got.at[1])
    wait_bytes(gv_in, TEAM - 1, got.at[4])

    grad_scale = 1.0 / math.sqrt(tok * n)
    all_gv = gv_in[...].reshape(TEAM * tok, gv.shape[1])
    for c in range(span // DH):
        h_cols = hid_in[:, :, c * DH : (c + 1) * DH].reshape(TEAM * tok, DH)
        part[c * DH : (c + 1) * DH, :] = dot(h_cols, all_gv, 0, 0) * grad_scale
    term_out[...] = part[...].reshape(teams, width, part.shape[1]).astype(BF16)
    for i in range(1, teams):
        other = lax.rem(team + i, teams)
        pltpu.make_async_remote_copy(
            term_out.at[other], term_in.at[team], sent.at[5], got.at[5],
            device_id=(other * TEAM + member,), device_id_type=MESH,
        ).start()

    wait_bytes(home, n - 1, got.at[3])

    def place(pair, c):
        at = pl.multiple_of(pair * 2 * ROWS, 2 * ROWS)
        for h in range(HK):
            both = [summed(home, 2 * pair + s, h, PER_KV * ROWS) for s in range(2)]
            dk_ref[pl.ds(at, 2 * ROWS), pl.ds(h * DH, DH)] = jnp.concatenate(
                both, axis=0
            ).astype(BF16)
            lower = home[HK * 2 * pair + h, 0 : PER_KV * ROWS, :].astype(F32)
            upper = home[HK * (2 * pair + 1) + h, 0 : PER_KV * ROWS, :].astype(F32)
            for i in range(PER_KV):
                cut = slice(i * ROWS, (i + 1) * ROWS)
                dq_ref[pl.ds(at, 2 * ROWS), pl.ds((PER_KV * h + i) * DH, DH)] = jnp.concatenate(
                    [lower[cut], upper[cut]], axis=0
                ).astype(BF16)
        return c

    lax.fori_loop(0, groups // 2, place, 0)

    wait_bytes(term_in, teams - 1, got.at[5])
    total = part[pl.ds(pl.multiple_of(team * width, width), width), :]
    for i in range(1, teams):
        total += term_in[lax.rem(team + i, teams)].astype(F32)
    dw_ref[...] = total

    wait_bytes(stage, n - 1, sent.at[0])
    wait_bytes(hid_out, TEAM - 1, sent.at[1])
    wait_bytes(back_v, n - 1, sent.at[2])
    wait_bytes(back, n - 1, sent.at[3])
    wait_bytes(gv_in, TEAM - 1, sent.at[4])
    wait_bytes(term_out, teams - 1, sent.at[5])


def local(hidden_in, queries, keys, values, grad_attn, send_rows, slot_docs):
    n = lax.axis_size("dp")
    tok, model = hidden_in.shape
    width = model // n
    teams = n // TEAM
    span = model // TEAM
    kv = keys.shape[1]
    if width % DH:
        hidden_in = (
            hidden_in.reshape(tok, teams, TEAM, width).swapaxes(1, 2).reshape(tok, model)
        )
    vmem = pl.BlockSpec(memory_space=pltpu.VMEM)
    smem = pl.BlockSpec(memory_space=pltpu.SMEM)
    owned = 2 * ROWS
    return pl.pallas_call(
        functools.partial(kernel, n, width),
        out_shape=(
            jax.ShapeDtypeStruct(queries.shape, BF16),
            jax.ShapeDtypeStruct(keys.shape, BF16),
            jax.ShapeDtypeStruct(values.shape, BF16),
            jax.ShapeDtypeStruct((width, kv), F32),
        ),
        in_specs=[vmem] * 6 + [smem],
        out_specs=(vmem,) * 4,
        scratch_shapes=[
            pltpu.VMEM(queries.shape, F32),
            pltpu.VMEM(queries.shape, F32),
            pltpu.VMEM((tok + ROWS, kv), F32),
            pltpu.VMEM((tok + ROWS, kv), F32),
            pltpu.VMEM((n, IN_ROWS, DH), BF16),
            pltpu.VMEM((n, IN_ROWS, DH), BF16),
            pltpu.VMEM((n * PER_KV * ROWS if n <= 64 else ROWS, n * owned), F32),
            pltpu.VMEM((n * owned, DH), F32),
            pltpu.VMEM((n * owned, DH), F32),
            pltpu.VMEM((n, owned, DH), BF16),
            pltpu.VMEM((n + HK, owned, DH), BF16),
            pltpu.VMEM((n, BACK_ROWS, DH), BF16),
            pltpu.VMEM((n + HK, BACK_ROWS, DH), BF16),
            pltpu.VMEM((TEAM, tok, span), BF16),
            pltpu.VMEM((TEAM, tok, span), BF16),
            pltpu.VMEM((tok, kv), BF16),
            pltpu.VMEM((TEAM, tok, kv), BF16),
            pltpu.VMEM((span, kv), F32),
            pltpu.VMEM((teams, width, kv), BF16),
            pltpu.VMEM((teams, width, kv), BF16),
            pltpu.SemaphoreType.DMA((6,)),
            pltpu.SemaphoreType.DMA((6,)),
        ],
        compiler_params=pltpu.CompilerParams(
            collective_id=0,
            has_side_effects=True,
            vmem_limit_bytes=(60 if n > 64 else 40) * 2**20,
        ),
    )(hidden_in, queries, keys, values, grad_attn, send_rows, slot_docs)


def solution(mesh):
    placed = (
        P("dp", None),
        P("dp", None),
        P("dp", None),
        P("dp", None),
        P("dp", None),
        P(),
        P("dp", None),
    )
    return jax.shard_map(
        local,
        mesh=mesh,
        in_specs=placed,
        out_specs=(P("dp", None), P("dp", None), P("dp", None), P("dp", None)),
        check_vma=False,
    )
```

```python
import functools
import math

import jax
import jax.numpy as jnp
from jax import lax
from jax.experimental import pallas as pl
from jax.experimental.pallas import tpu as pltpu
from jax.sharding import PartitionSpec as P

HQ = 16
HK = 4
DH = 128
PER_KV = HQ // HK
ROWS = 8
HALO = 3
TEAM = 8
MESH = pl.DeviceIdType.MESH
F32 = jnp.float32
BF16 = jnp.bfloat16

HEAD_ROWS = PER_KV * ROWS
MSG_ROWS = HEAD_ROWS + 2 * ROWS


def dot(a, b, da, db):
    return lax.dot_general(a, b, (((da,), (db,)), ((), ())), preferred_element_type=F32)


def wait_bytes(ref, count, sem):
    view = ref.at[pl.ds(0, count)]
    pltpu.make_async_copy(view, view, sem).wait()


def kernel(
    n, width,
    hid_hbm, q_hbm, k_hbm, v_hbm, o_hbm, rows_hbm, docs_hbm,
    dq_hbm, dk_hbm, dv_hbm, dw_hbm,
    hid_ref, q_ref, k_ref, v_ref, o_ref, rows_ref, docs_ref, dq_ref, dk_ref, dw_ref,
    q32, o32, k32, v32, stage_s, came_s, stage_g, came_g, probs, acc_v, acc_k,
    back_v, home_v, back, home, hid_out, hid_in, hid_t, gv, gv_in, term_out, term_in,
    loaded, stored, sent, got,
):
    me = lax.axis_index("dp")
    tok = q_ref.shape[0]
    groups = n // HK
    teams = n // TEAM
    member = lax.rem(me, TEAM)
    team = lax.div(me, TEAM)
    group = lax.div(me, HK)
    scale = 1.0 / math.sqrt(DH)
    keys = n * 2 * ROWS
    chunk = 8
    q_rows = chunk * PER_KV * ROWS

    loads = [
        pltpu.make_async_copy(src, dst, loaded.at[i])
        for i, (src, dst) in enumerate(
            (
                (q_hbm, q_ref),
                (k_hbm, k_ref),
                (docs_hbm, docs_ref),
                (o_hbm, o_ref),
                (v_hbm, v_ref),
                (hid_hbm, hid_ref),
                (rows_hbm, rows_ref),
            )
        )
    ]
    for load in loads:
        load.start()

    barrier = pltpu.get_barrier_semaphore()

    def greet(i, c):
        pl.semaphore_signal(
            barrier, inc=1, device_id=(lax.rem(me + i, n),), device_id_type=MESH
        )
        return c

    lax.fori_loop(1, n, greet, 0)

    k32[0:ROWS, :] = jnp.zeros((ROWS, k32.shape[1]), F32)
    v32[0:ROWS, :] = jnp.zeros((ROWS, v32.shape[1]), F32)
    for load in loads[:3]:
        load.wait()
    q32[...] = q_ref[...].astype(F32)
    k32[ROWS:, :] = k_ref[...].astype(F32)
    lane = lax.broadcasted_iota(jnp.int32, (2 * ROWS, DH), 1)
    line = lax.broadcasted_iota(jnp.int32, (2 * ROWS, DH), 0)
    doc_line = jnp.zeros((2 * ROWS, DH), F32)
    for j in range(docs_ref.shape[1]):
        doc_line = jnp.where(lane == j, (docs_ref[0, j] + 1).astype(F32), doc_line)

    def packer(dst, heads, tail, with_docs):
        def pack(g, c):
            at = pl.multiple_of(g * ROWS, ROWS)
            for h in range(HK):
                parts = [
                    heads[pl.ds(at, ROWS), pl.ds((PER_KV * h + i) * DH, DH)]
                    for i in range(PER_KV)
                ]
                part = tail[pl.ds(at, 2 * ROWS), pl.ds(h * DH, DH)]
                parts.append(jnp.where(line == 0, doc_line, part) if with_docs else part)
                dst[HK * g + h] = jnp.concatenate(parts, axis=0).astype(BF16)
            return c

        return pack

    def to_all(src, dst, index):
        def send(i, c):
            peer = lax.rem(me + i * (TEAM + 1), n)
            pltpu.make_async_remote_copy(
                src.at[peer], dst.at[me], sent.at[index], got.at[index],
                device_id=(peer,), device_id_type=MESH,
            ).start()
            return c

        lax.fori_loop(1, n, send, 0)

    def to_team(src_of, dst, index):
        for i in range(1, TEAM):
            other = lax.rem(member + i, TEAM)
            pltpu.make_async_remote_copy(
                src_of(other), dst.at[member], sent.at[index], got.at[index],
                device_id=(team * TEAM + other,), device_id_type=MESH,
            ).start()

    lax.fori_loop(0, groups, packer(stage_s, q32, k32, True), 0)
    pl.semaphore_wait(barrier, n - 1)
    to_all(stage_s, came_s, 0)

    for load in loads[3:5]:
        load.wait()
    o32[...] = o_ref[...].astype(F32)
    v32[ROWS:, :] = v_ref[...].astype(F32)
    lax.fori_loop(0, groups, packer(stage_g, o32, v32, False), 0)
    to_all(stage_g, came_g, 6)

    for load in loads[5:]:
        load.wait()
    span = hid_out.shape[2]
    for m in range(TEAM):
        if width % DH == 0:
            for p in range(teams):
                hid_out[m, :, p * width : (p + 1) * width] = hid_ref[
                    :, (p * TEAM + m) * width : (p * TEAM + m + 1) * width
                ]
        else:
            hid_out[m] = hid_ref[:, m * span : (m + 1) * span]
    to_team(lambda other: hid_out.at[other], hid_in, 1)
    hid_in[member] = hid_out[member]

    came_s[me] = stage_s[me]
    came_g[me] = stage_g[me]
    acc_v[...] = jnp.zeros_like(acc_v)
    acc_k[...] = jnp.zeros_like(acc_k)
    home_v[n:, :, :] = jnp.zeros((HK, 2 * ROWS, DH), BF16)
    home[n:, :, :] = jnp.zeros((HK, MSG_ROWS, DH), BF16)

    wait_bytes(came_s, n - 1, got.at[0])

    doc_rows = came_s[:, HEAD_ROWS:, :][:, 0, :]
    pick = (
        lax.broadcasted_iota(jnp.int32, (8, DH), 0) == lax.broadcasted_iota(jnp.int32, (8, DH), 1)
    ).astype(F32).astype(BF16)
    doc_table = dot(pick, doc_rows, 1, 1)
    loc = lax.broadcasted_iota(jnp.int32, (2 * ROWS, n), 0) + (group - 1) * ROWS
    doc_sum = jnp.zeros((2 * ROWS, n), F32)
    for j in range(rows_ref.shape[0]):
        doc_sum += jnp.where(rows_ref[j : j + 1, :] == loc, doc_table[j : j + 1, :], 0.0)
    docs = jnp.sum(doc_sum, axis=1, keepdims=True)
    own_docs = docs[ROWS:]
    back_count = jnp.zeros((ROWS, 1), F32)
    for d in range(1, HALO + 1):
        back_count += jnp.where(docs[ROWS - d : 2 * ROWS - d] == own_docs, 1.0, 0.0)
    first = (
        lax.broadcasted_iota(jnp.int32, (ROWS, 1), 0) - back_count.astype(jnp.int32)
    ) * n
    first = jnp.broadcast_to(first[None], (q_rows // ROWS, ROWS, 1)).reshape(q_rows, 1)
    col = lax.broadcasted_iota(jnp.int32, (1, keys), 1)
    k_pos = (lax.rem(col, 2 * ROWS) - ROWS) * n + lax.div(col, 2 * ROWS)
    row = lax.broadcasted_iota(jnp.int32, (q_rows, 1), 0)
    q_pos = lax.rem(row, ROWS) * n + lax.div(row, HEAD_ROWS)

    def rows_of(ref, c):
        return ref[pl.ds(c * chunk, chunk), 0:HEAD_ROWS, :].reshape(q_rows, DH)

    def keys_of(ref):
        return ref[:, HEAD_ROWS:, :].reshape(keys, DH)

    def prob_of(c):
        scores = dot(rows_of(came_s, c), keys_of(came_s), 1, 1) * scale
        allowed = (k_pos >= first) & (k_pos <= q_pos + c * chunk)
        scores = jnp.where(allowed, scores, -1000000000.0)
        weights = jnp.exp(scores - jnp.max(scores, axis=1, keepdims=True))
        return weights * (1.0 / jnp.sum(weights, axis=1, keepdims=True))

    kept = probs.shape[0] > q_rows

    def prob_rows(c):
        return pl.ds(pl.multiple_of(c * q_rows, q_rows), q_rows)

    def soft(c, carry):
        probs[prob_rows(c), :] = prob_of(c)
        return carry

    if kept:
        lax.fori_loop(0, n // chunk, soft, 0)

    wait_bytes(came_g, n - 1, got.at[6])

    def value_grads(c, carry):
        p = probs[prob_rows(c), :] if kept else prob_of(c)
        acc_v[...] += dot(p.astype(BF16), rows_of(came_g, c), 0, 0)
        return carry

    lax.fori_loop(0, n // chunk, value_grads, 0)
    back_v[...] = acc_v[...].reshape(n, 2 * ROWS, DH).astype(BF16)
    to_all(back_v, home_v, 2)
    home_v[me] = back_v[me]

    def grads(c, carry):
        p = probs[prob_rows(c), :] if kept else prob_of(c)
        dprob = dot(rows_of(came_g, c), keys_of(came_g), 1, 1)
        delta = jnp.sum(p * dprob, axis=1, keepdims=True)
        dscore = (p * (dprob - delta) * scale).astype(BF16)
        dq = dot(dscore, keys_of(came_s), 1, 0).astype(BF16)
        back[pl.ds(c * chunk, chunk), 0:HEAD_ROWS, :] = dq.reshape(chunk, HEAD_ROWS, DH)
        acc_k[...] += dot(dscore, rows_of(came_s, c), 0, 0)
        return carry

    lax.fori_loop(0, n // chunk, grads, 0)
    back[:, HEAD_ROWS:, :] = acc_k[...].reshape(n, 2 * ROWS, DH).astype(BF16)
    to_all(back, home, 3)
    home[me] = back[me]

    wait_bytes(hid_in, TEAM - 1, got.at[1])
    tile = DH // min(tok, DH)
    for t in range(TEAM * tok // DH):
        if tile > 1:
            rows = hid_in[t * tile : (t + 1) * tile].reshape(DH, span)
        else:
            per = tok // DH
            rows = hid_in[t // per, (t % per) * DH : (t % per + 1) * DH, :]
        hid_t[:, t * DH : (t + 1) * DH] = rows.T

    def summed(ref, g, h, at):
        own = ref[HK * g + h, at : at + 2 * ROWS, :].astype(F32)
        after = ref[HK * g + HK + h, at : at + 2 * ROWS, :].astype(F32)
        return own[ROWS:] + after[:ROWS]

    wait_bytes(home_v, n - 1, got.at[2])

    def place_v(pair, c):
        at = pl.multiple_of(pair * 2 * ROWS, 2 * ROWS)
        for h in range(HK):
            both = [summed(home_v, 2 * pair + s, h, 0) for s in range(2)]
            gv[pl.ds(at, 2 * ROWS), pl.ds(h * DH, DH)] = jnp.concatenate(both, axis=0).astype(BF16)
        return c

    lax.fori_loop(0, groups // 2, place_v, 0)
    to_team(lambda other: gv, gv_in, 4)
    store_v = pltpu.make_async_copy(gv, dv_hbm, stored.at[0])
    store_v.start()
    gv_in[member] = gv[...]
    wait_bytes(gv_in, TEAM - 1, got.at[4])

    grad_scale = 1.0 / math.sqrt(tok * n)

    def term(p):
        cols = hid_t[pl.ds(pl.multiple_of(p * width, width), width), :]
        return dot(cols, gv_in[...].reshape(TEAM * tok, gv.shape[1]), 1, 0) * grad_scale

    for i in range(1, teams):
        other = lax.rem(team + i, teams)
        term_out[other] = term(other).astype(BF16)
        pltpu.make_async_remote_copy(
            term_out.at[other], term_in.at[team], sent.at[5], got.at[5],
            device_id=(other * TEAM + member,), device_id_type=MESH,
        ).start()
    dw_ref[...] = term(team)

    wait_bytes(home, n - 1, got.at[3])

    def place(pair, c):
        at = pl.multiple_of(pair * 2 * ROWS, 2 * ROWS)
        for h in range(HK):
            both = [summed(home, 2 * pair + s, h, HEAD_ROWS) for s in range(2)]
            dk_ref[pl.ds(at, 2 * ROWS), pl.ds(h * DH, DH)] = jnp.concatenate(
                both, axis=0
            ).astype(BF16)
            lower = home[HK * 2 * pair + h, 0:HEAD_ROWS, :].astype(F32)
            upper = home[HK * (2 * pair + 1) + h, 0:HEAD_ROWS, :].astype(F32)
            for i in range(PER_KV):
                cut = slice(i * ROWS, (i + 1) * ROWS)
                dq_ref[pl.ds(at, 2 * ROWS), pl.ds((PER_KV * h + i) * DH, DH)] = jnp.concatenate(
                    [lower[cut], upper[cut]], axis=0
                ).astype(BF16)
        return c

    lax.fori_loop(0, groups // 2, place, 0)
    store_q = pltpu.make_async_copy(dq_ref, dq_hbm, stored.at[1])
    store_k = pltpu.make_async_copy(dk_ref, dk_hbm, stored.at[2])
    store_q.start()
    store_k.start()

    wait_bytes(term_in, teams - 1, got.at[5])
    total = dw_ref[...]
    for i in range(1, teams):
        total += term_in[lax.rem(team + i, teams)].astype(F32)
    dw_ref[...] = total
    store_w = pltpu.make_async_copy(dw_ref, dw_hbm, stored.at[3])
    store_w.start()

    wait_bytes(stage_s, n - 1, sent.at[0])
    wait_bytes(stage_g, n - 1, sent.at[6])
    wait_bytes(hid_out, TEAM - 1, sent.at[1])
    wait_bytes(back_v, n - 1, sent.at[2])
    wait_bytes(back, n - 1, sent.at[3])
    wait_bytes(gv_in, TEAM - 1, sent.at[4])
    wait_bytes(term_out, teams - 1, sent.at[5])
    store_v.wait()
    store_q.wait()
    store_k.wait()
    store_w.wait()


def hand_over(*refs):
    count = (len(refs) - 2) // 3
    srcs, dsts, held = refs[:count], refs[count : 2 * count], refs[2 * count : 3 * count]
    in_sem, out_sem = refs[3 * count :]
    ins = [pltpu.make_async_copy(srcs[i], held[i], in_sem.at[i]) for i in range(count)]
    outs = [pltpu.make_async_copy(held[i], dsts[i], out_sem.at[i]) for i in range(count)]
    for copy in ins:
        copy.start()
    for i in range(count):
        ins[i].wait()
        outs[i].start()
    for copy in outs:
        copy.wait()


def local(hidden_in, queries, keys, values, grad_attn, send_rows, slot_docs):
    n = lax.axis_size("dp")
    tok, model = hidden_in.shape
    width = model // n
    teams = n // TEAM
    span = model // TEAM
    kv = keys.shape[1]
    if width % DH:
        hidden_in = (
            hidden_in.reshape(tok, teams, TEAM, width).swapaxes(1, 2).reshape(tok, model)
        )
    whole = pl.BlockSpec(memory_space=pl.ANY)
    owned = 2 * ROWS
    results = (
        jax.ShapeDtypeStruct(queries.shape, BF16),
        jax.ShapeDtypeStruct(keys.shape, BF16),
        jax.ShapeDtypeStruct(values.shape, BF16),
        jax.ShapeDtypeStruct((width, kv), F32),
    )
    outs = pl.pallas_call(
        functools.partial(kernel, n, width),
        out_shape=results,
        in_specs=[whole] * 7,
        out_specs=(whole,) * 4,
        scratch_shapes=[
            pltpu.VMEM(hidden_in.shape, BF16),
            pltpu.VMEM(queries.shape, BF16),
            pltpu.VMEM(keys.shape, BF16),
            pltpu.VMEM(values.shape, BF16),
            pltpu.VMEM(grad_attn.shape, BF16),
            pltpu.VMEM(send_rows.shape, jnp.int32),
            pltpu.SMEM(slot_docs.shape, jnp.int32),
            pltpu.VMEM(queries.shape, BF16),
            pltpu.VMEM(keys.shape, BF16),
            pltpu.VMEM((width, kv), F32),
            pltpu.VMEM(queries.shape, F32),
            pltpu.VMEM(queries.shape, F32),
            pltpu.VMEM((tok + ROWS, kv), F32),
            pltpu.VMEM((tok + ROWS, kv), F32),
            pltpu.VMEM((n, MSG_ROWS, DH), BF16),
            pltpu.VMEM((n, MSG_ROWS, DH), BF16),
            pltpu.VMEM((n, MSG_ROWS, DH), BF16),
            pltpu.VMEM((n, MSG_ROWS, DH), BF16),
            pltpu.VMEM((n * HEAD_ROWS if n <= 64 else ROWS, n * owned), F32),
            pltpu.VMEM((n * owned, DH), F32),
            pltpu.VMEM((n * owned, DH), F32),
            pltpu.VMEM((n, owned, DH), BF16),
            pltpu.VMEM((n + HK, owned, DH), BF16),
            pltpu.VMEM((n, MSG_ROWS, DH), BF16),
            pltpu.VMEM((n + HK, MSG_ROWS, DH), BF16),
            pltpu.VMEM((TEAM, tok, span), BF16),
            pltpu.VMEM((TEAM, tok, span), BF16),
            pltpu.VMEM((span, TEAM * tok), BF16),
            pltpu.VMEM((tok, kv), BF16),
            pltpu.VMEM((TEAM, tok, kv), BF16),
            pltpu.VMEM((teams, width, kv), BF16),
            pltpu.VMEM((teams, width, kv), BF16),
            pltpu.SemaphoreType.DMA((7,)),
            pltpu.SemaphoreType.DMA((4,)),
            pltpu.SemaphoreType.DMA((7,)),
            pltpu.SemaphoreType.DMA((7,)),
        ],
        compiler_params=pltpu.CompilerParams(
            collective_id=0, has_side_effects=True, vmem_limit_bytes=62 * 2**20
        ),
    )(hidden_in, queries, keys, values, grad_attn, send_rows, slot_docs)
    return pl.pallas_call(
        hand_over,
        out_shape=results,
        in_specs=[whole] * 4,
        out_specs=(whole,) * 4,
        scratch_shapes=[
            *(pltpu.VMEM(out.shape, out.dtype) for out in results),
            pltpu.SemaphoreType.DMA((4,)),
            pltpu.SemaphoreType.DMA((4,)),
        ],
        compiler_params=pltpu.CompilerParams(vmem_limit_bytes=62 * 2**20),
    )(*outs)


def solution(mesh):
    placed = (
        P("dp", None),
        P("dp", None),
        P("dp", None),
        P("dp", None),
        P("dp", None),
        P(),
        P("dp", None),
    )
    return jax.shard_map(
        local,
        mesh=mesh,
        in_specs=placed,
        out_specs=(P("dp", None), P("dp", None), P("dp", None), P("dp", None)),
        check_vma=False,
    )
```

```python
import functools
import math

import jax
import jax.numpy as jnp
from jax import lax
from jax.experimental import pallas as pl
from jax.experimental.pallas import tpu as pltpu
from jax.sharding import PartitionSpec as P

HQ = 16
HK = 4
DH = 128
PER_KV = HQ // HK
ROWS = 8
HALO = 3
TEAM = 16
PARTS = 2
MESH = pl.DeviceIdType.MESH
F32 = jnp.float32
BF16 = jnp.bfloat16

HEAD_ROWS = PER_KV * ROWS
MSG_ROWS = HEAD_ROWS + 2 * ROWS


def dot(a, b, da, db):
    return lax.dot_general(a, b, (((da,), (db,)), ((), ())), preferred_element_type=F32)


def wait_bytes(ref, count, sem):
    view = ref.at[pl.ds(0, count)]
    pltpu.make_async_copy(view, view, sem).wait()


def kernel(
    n, width,
    hid_hbm, q_hbm, k_hbm, v_hbm, o_hbm, rows_hbm, docs_hbm,
    dq_hbm, dk_hbm, dv_hbm, dw_hbm,
    hid_ref, q_ref, k_ref, v_ref, o_ref, rows_ref, docs_ref, dq_ref, dk_ref, dw_ref,
    q32, o32, k32, v32, stage_s, came_s, stage_g, came_g, probs, acc_v, acc_k,
    back_v, home_v, back, home, hid_out, hid_in, hid_t, gv, gv_in, terms, term_out, term_in,
    loaded, stored, sent, got, near, near_got,
):
    me = lax.axis_index("dp")
    tok = q_ref.shape[0]
    groups = n // HK
    teams = n // TEAM
    member = lax.rem(me, TEAM)
    team = lax.div(me, TEAM)
    core = lax.rem(me, 2)
    spot = lax.rem(lax.div(me, 2), 4)
    side = lax.rem(lax.div(me, 8), 2)

    def place_in_team(a_core, a_side, a_spot):
        return a_core * 8 + a_side * 4 + a_spot

    def place_of(a_member):
        return place_in_team(
            lax.rem(a_member, 2), lax.div(a_member, 8), lax.rem(lax.div(a_member, 2), 4)
        )

    my_place = place_in_team(core, side, spot)

    def device_at(a_core, a_side, a_spot):
        return team * TEAM + a_side * 8 + a_spot * 2 + a_core

    group = lax.div(me, HK)
    scale = 1.0 / math.sqrt(DH)
    keys = n * 2 * ROWS
    chunk = 8
    q_rows = chunk * PER_KV * ROWS

    loads = [
        pltpu.make_async_copy(src, dst, loaded.at[i])
        for i, (src, dst) in enumerate(
            (
                (q_hbm, q_ref),
                (k_hbm, k_ref),
                (docs_hbm, docs_ref),
                (o_hbm, o_ref),
                (v_hbm, v_ref),
                (hid_hbm, hid_ref),
                (rows_hbm, rows_ref),
            )
        )
    ]
    for load in loads:
        load.start()

    barrier = pltpu.get_barrier_semaphore()

    def greet(i, c):
        pl.semaphore_signal(
            barrier, inc=1, device_id=(lax.rem(me + i, n),), device_id_type=MESH
        )
        return c

    lax.fori_loop(1, n, greet, 0)

    k32[0:ROWS, :] = jnp.zeros((ROWS, k32.shape[1]), F32)
    v32[0:ROWS, :] = jnp.zeros((ROWS, v32.shape[1]), F32)
    for load in loads[:3]:
        load.wait()
    q32[...] = q_ref[...].astype(F32)
    k32[ROWS:, :] = k_ref[...].astype(F32)
    lane = lax.broadcasted_iota(jnp.int32, (2 * ROWS, DH), 1)
    line = lax.broadcasted_iota(jnp.int32, (2 * ROWS, DH), 0)
    doc_line = jnp.zeros((2 * ROWS, DH), F32)
    for j in range(docs_ref.shape[1]):
        doc_line = jnp.where(lane == j, (docs_ref[0, j] + 1).astype(F32), doc_line)

    def packer(dst, heads, tail, with_docs):
        def pack(g, c):
            at = pl.multiple_of(g * ROWS, ROWS)
            for h in range(HK):
                parts = [
                    heads[pl.ds(at, ROWS), pl.ds((PER_KV * h + i) * DH, DH)]
                    for i in range(PER_KV)
                ]
                part = tail[pl.ds(at, 2 * ROWS), pl.ds(h * DH, DH)]
                parts.append(jnp.where(line == 0, doc_line, part) if with_docs else part)
                dst[HK * g + h] = jnp.concatenate(parts, axis=0).astype(BF16)
            return c

        return pack

    def to_all(src, dst, index):
        def send(i, c):
            peer = lax.rem(me + i * 9, n)
            pltpu.make_async_remote_copy(
                src.at[peer], dst.at[me], sent.at[index], got.at[index],
                device_id=(peer,), device_id_type=MESH,
            ).start()
            return c

        lax.fori_loop(1, n, send, 0)

    lax.fori_loop(0, groups, packer(stage_s, q32, k32, True), 0)
    pl.semaphore_wait(barrier, n - 1)
    to_all(stage_s, came_s, 0)

    for load in loads[3:5]:
        load.wait()
    o32[...] = o_ref[...].astype(F32)
    v32[ROWS:, :] = v_ref[...].astype(F32)
    lax.fori_loop(0, groups, packer(stage_g, o32, v32, False), 0)
    to_all(stage_g, came_g, 6)

    for load in loads[5:]:
        load.wait()
    span = hid_out.shape[2]
    for m in range(TEAM):
        if width % DH == 0:
            for p in range(teams):
                hid_out[m, :, p * width : (p + 1) * width] = hid_ref[
                    :, (p * TEAM + m) * width : (p * TEAM + m + 1) * width
                ]
        else:
            hid_out[m] = hid_ref[:, m * span : (m + 1) * span]
    for i in range(1, TEAM):
        other = lax.rem(member + i, TEAM)
        pltpu.make_async_remote_copy(
            hid_out.at[other], hid_in.at[my_place], sent.at[1], got.at[1],
            device_id=(team * TEAM + other,), device_id_type=MESH,
        ).start()
    hid_in[my_place] = hid_out[member]

    came_s[me] = stage_s[me]
    came_g[me] = stage_g[me]
    acc_v[...] = jnp.zeros_like(acc_v)
    acc_k[...] = jnp.zeros_like(acc_k)
    home_v[n:, :, :] = jnp.zeros((HK, 2 * ROWS, DH), BF16)
    home[n:, :, :] = jnp.zeros((HK, MSG_ROWS, DH), BF16)

    wait_bytes(came_s, n - 1, got.at[0])

    doc_rows = came_s[:, HEAD_ROWS:, :][:, 0, :]
    pick = (
        lax.broadcasted_iota(jnp.int32, (8, DH), 0) == lax.broadcasted_iota(jnp.int32, (8, DH), 1)
    ).astype(F32).astype(BF16)
    doc_table = dot(pick, doc_rows, 1, 1)
    loc = lax.broadcasted_iota(jnp.int32, (2 * ROWS, n), 0) + (group - 1) * ROWS
    doc_sum = jnp.zeros((2 * ROWS, n), F32)
    for j in range(rows_ref.shape[0]):
        doc_sum += jnp.where(rows_ref[j : j + 1, :] == loc, doc_table[j : j + 1, :], 0.0)
    docs = jnp.sum(doc_sum, axis=1, keepdims=True)
    own_docs = docs[ROWS:]
    back_count = jnp.zeros((ROWS, 1), F32)
    for d in range(1, HALO + 1):
        back_count += jnp.where(docs[ROWS - d : 2 * ROWS - d] == own_docs, 1.0, 0.0)
    first = (
        lax.broadcasted_iota(jnp.int32, (ROWS, 1), 0) - back_count.astype(jnp.int32)
    ) * n
    first = jnp.broadcast_to(first[None], (q_rows // ROWS, ROWS, 1)).reshape(q_rows, 1)
    col = lax.broadcasted_iota(jnp.int32, (1, keys), 1)
    k_pos = (lax.rem(col, 2 * ROWS) - ROWS) * n + lax.div(col, 2 * ROWS)
    row = lax.broadcasted_iota(jnp.int32, (q_rows, 1), 0)
    q_pos = lax.rem(row, ROWS) * n + lax.div(row, HEAD_ROWS)

    def rows_of(ref, c):
        return ref[pl.ds(c * chunk, chunk), 0:HEAD_ROWS, :].reshape(q_rows, DH)

    def keys_of(ref):
        return ref[:, HEAD_ROWS:, :].reshape(keys, DH)

    def prob_of(c):
        scores = dot(rows_of(came_s, c), keys_of(came_s), 1, 1) * scale
        allowed = (k_pos >= first) & (k_pos <= q_pos + c * chunk)
        scores = jnp.where(allowed, scores, -1000000000.0)
        weights = jnp.exp(scores - jnp.max(scores, axis=1, keepdims=True))
        return weights * (1.0 / jnp.sum(weights, axis=1, keepdims=True))

    kept = probs.shape[0] > q_rows

    def prob_rows(c):
        return pl.ds(pl.multiple_of(c * q_rows, q_rows), q_rows)

    def soft(c, carry):
        probs[prob_rows(c), :] = prob_of(c)
        return carry

    if kept:
        lax.fori_loop(0, n // chunk, soft, 0)

    wait_bytes(came_g, n - 1, got.at[6])

    def value_grads(c, carry):
        p = probs[prob_rows(c), :] if kept else prob_of(c)
        acc_v[...] += dot(p.astype(BF16), rows_of(came_g, c), 0, 0)
        return carry

    lax.fori_loop(0, n // chunk, value_grads, 0)
    back_v[...] = acc_v[...].reshape(n, 2 * ROWS, DH).astype(BF16)
    to_all(back_v, home_v, 2)
    home_v[me] = back_v[me]

    def grads(c, carry):
        p = probs[prob_rows(c), :] if kept else prob_of(c)
        dprob = dot(rows_of(came_g, c), keys_of(came_g), 1, 1)
        delta = jnp.sum(p * dprob, axis=1, keepdims=True)
        dscore = (p * (dprob - delta) * scale).astype(BF16)
        dq = dot(dscore, keys_of(came_s), 1, 0).astype(BF16)
        back[pl.ds(c * chunk, chunk), 0:HEAD_ROWS, :] = dq.reshape(chunk, HEAD_ROWS, DH)
        acc_k[...] += dot(dscore, rows_of(came_s, c), 0, 0)
        return carry

    lax.fori_loop(0, n // chunk, grads, 0)
    back[:, HEAD_ROWS:, :] = acc_k[...].reshape(n, 2 * ROWS, DH).astype(BF16)
    wait_bytes(hid_in, TEAM - 1, got.at[1])
    tile = DH // min(tok, DH)
    for t in range(TEAM * tok // DH):
        if tile > 1:
            rows = hid_in[t * tile : (t + 1) * tile].reshape(DH, span)
        else:
            per = tok // DH
            rows = hid_in[t // per, (t % per) * DH : (t % per + 1) * DH, :]
        hid_t[:, t * DH : (t + 1) * DH] = rows.T

    def summed(ref, g, h, at):
        own = ref[HK * g + h, at : at + 2 * ROWS, :].astype(F32)
        after = ref[HK * g + HK + h, at : at + 2 * ROWS, :].astype(F32)
        return own[ROWS:] + after[:ROWS]

    wait_bytes(home_v, n - 1, got.at[2])

    def place_v(pair, c):
        at = pl.multiple_of(pair * 2 * ROWS, 2 * ROWS)
        for h in range(HK):
            both = [summed(home_v, 2 * pair + s, h, 0) for s in range(2)]
            gv[pl.ds(at, 2 * ROWS), pl.ds(h * DH, DH)] = jnp.concatenate(both, axis=0).astype(BF16)
        return c

    lax.fori_loop(0, groups // 2, place_v, 0)

    def pass_on(src, place, device, send_sem, recv_sem):
        pltpu.make_async_remote_copy(
            src, gv_in.at[place], send_sem, recv_sem,
            device_id=(device,), device_id_type=MESH,
        ).start()

    partner_place = place_in_team(core, 1 - side, spot)
    sibling = device_at(1 - core, side, spot)
    pass_on(gv, my_place, device_at(core, 1 - side, spot), near.at[0], near_got.at[0])
    for i in range(1, 4):
        there = device_at(core, side, lax.rem(spot + i, 4))
        pass_on(gv, my_place, there, near.at[i], near_got.at[i])
    pass_on(gv, my_place, sibling, sent.at[4], got.at[4])
    store_v = pltpu.make_async_copy(gv, dv_hbm, stored.at[0])
    store_v.start()
    to_all(back, home, 3)
    home[me] = back[me]
    gv_in[my_place] = gv[...]

    def landed(i):
        pltpu.make_async_copy(gv, gv, near_got.at[i]).wait()

    def across(place):
        pass_on(gv_in.at[place], place, sibling, sent.at[4], got.at[4])

    landed(0)
    for i in range(1, 4):
        there = device_at(core, side, lax.rem(spot + i, 4))
        pass_on(gv_in.at[partner_place], partner_place, there, near.at[3 + i], near_got.at[3 + i])
    across(partner_place)
    for i in range(1, 4):
        landed(i)
        across(place_in_team(core, side, lax.rem(spot + 4 - i, 4)))
    for i in range(1, 4):
        landed(3 + i)
        across(place_in_team(core, 1 - side, lax.rem(spot + 4 - i, 4)))

    grad_scale = 1.0 / math.sqrt(tok * n)
    half = TEAM // 2 * tok

    def half_term(p, which):
        cols = hid_t[
            pl.ds(pl.multiple_of(p * width, width), width),
            pl.ds(pl.multiple_of(which * half, half), half),
        ]
        rows = gv_in[pl.ds(which * (TEAM // 2), TEAM // 2)].reshape(half, gv.shape[1])
        return dot(cols, rows, 1, 0) * grad_scale

    for i in range(teams):
        other = lax.rem(team + i, teams)
        terms[i] = half_term(other, core)
    wait_bytes(gv_in, TEAM // 2, got.at[4])

    for i in range(1, teams):
        other = lax.rem(team + i, teams)
        term_out[other] = (terms[i] + half_term(other, 1 - core)).astype(BF16)
        pltpu.make_async_remote_copy(
            term_out.at[other], term_in.at[team], sent.at[5], got.at[5],
            device_id=(other * TEAM + member,), device_id_type=MESH,
        ).start()
    dw_ref[...] = terms[0] + half_term(team, 1 - core)

    wait_bytes(home, n - 1, got.at[3])

    def place(pair, c):
        at = pl.multiple_of(pair * 2 * ROWS, 2 * ROWS)
        for h in range(HK):
            both = [summed(home, 2 * pair + s, h, HEAD_ROWS) for s in range(2)]
            dk_ref[pl.ds(at, 2 * ROWS), pl.ds(h * DH, DH)] = jnp.concatenate(
                both, axis=0
            ).astype(BF16)
            lower = home[HK * 2 * pair + h, 0:HEAD_ROWS, :].astype(F32)
            upper = home[HK * (2 * pair + 1) + h, 0:HEAD_ROWS, :].astype(F32)
            for i in range(PER_KV):
                cut = slice(i * ROWS, (i + 1) * ROWS)
                dq_ref[pl.ds(at, 2 * ROWS), pl.ds((PER_KV * h + i) * DH, DH)] = jnp.concatenate(
                    [lower[cut], upper[cut]], axis=0
                ).astype(BF16)
        return c

    lax.fori_loop(0, groups // 2, place, 0)
    store_q = pltpu.make_async_copy(dq_ref, dq_hbm, stored.at[1])
    store_k = pltpu.make_async_copy(dk_ref, dk_hbm, stored.at[2])
    store_q.start()
    store_k.start()

    wait_bytes(term_in, teams - 1, got.at[5])
    total = dw_ref[...]
    for i in range(1, teams):
        total += term_in[lax.rem(team + i, teams)].astype(F32)
    dw_ref[...] = total
    store_w = pltpu.make_async_copy(dw_ref, dw_hbm, stored.at[3])
    store_w.start()

    wait_bytes(stage_s, n - 1, sent.at[0])
    wait_bytes(stage_g, n - 1, sent.at[6])
    wait_bytes(hid_out, TEAM - 1, sent.at[1])
    wait_bytes(back_v, n - 1, sent.at[2])
    wait_bytes(back, n - 1, sent.at[3])
    wait_bytes(gv_in, TEAM // 2, sent.at[4])
    for i in range(7):
        pltpu.make_async_copy(gv, gv, near.at[i]).wait()
    wait_bytes(term_out, teams - 1, sent.at[5])
    store_v.wait()
    store_q.wait()
    store_k.wait()
    store_w.wait()


def hand_over(*refs):
    count = len(refs) // 2
    sems = refs[-1]
    copies = []
    for src, dst in zip(refs[:count], refs[count : 2 * count]):
        rows = src.shape[0] // PARTS
        for p in range(PARTS):
            cut = pl.ds(p * rows, rows)
            copies.append(pltpu.make_async_copy(src.at[cut], dst.at[cut], sems.at[len(copies)]))
    for copy in copies:
        copy.start()
    for copy in copies:
        copy.wait()


def local(hidden_in, queries, keys, values, grad_attn, send_rows, slot_docs):
    n = lax.axis_size("dp")
    tok, model = hidden_in.shape
    width = model // n
    teams = n // TEAM
    span = model // TEAM
    kv = keys.shape[1]
    if width % DH:
        hidden_in = (
            hidden_in.reshape(tok, teams, TEAM, width).swapaxes(1, 2).reshape(tok, model)
        )
    whole = pl.BlockSpec(memory_space=pl.ANY)
    owned = 2 * ROWS
    results = (
        jax.ShapeDtypeStruct(queries.shape, BF16),
        jax.ShapeDtypeStruct(keys.shape, BF16),
        jax.ShapeDtypeStruct(values.shape, BF16),
        jax.ShapeDtypeStruct((width, kv), F32),
    )
    outs = pl.pallas_call(
        functools.partial(kernel, n, width),
        out_shape=results,
        in_specs=[whole] * 7,
        out_specs=(whole,) * 4,
        scratch_shapes=[
            pltpu.VMEM(hidden_in.shape, BF16),
            pltpu.VMEM(queries.shape, BF16),
            pltpu.VMEM(keys.shape, BF16),
            pltpu.VMEM(values.shape, BF16),
            pltpu.VMEM(grad_attn.shape, BF16),
            pltpu.VMEM(send_rows.shape, jnp.int32),
            pltpu.SMEM(slot_docs.shape, jnp.int32),
            pltpu.VMEM(queries.shape, BF16),
            pltpu.VMEM(keys.shape, BF16),
            pltpu.VMEM((width, kv), F32),
            pltpu.VMEM(queries.shape, F32),
            pltpu.VMEM(queries.shape, F32),
            pltpu.VMEM((tok + ROWS, kv), F32),
            pltpu.VMEM((tok + ROWS, kv), F32),
            pltpu.VMEM((n, MSG_ROWS, DH), BF16),
            pltpu.VMEM((n, MSG_ROWS, DH), BF16),
            pltpu.VMEM((n, MSG_ROWS, DH), BF16),
            pltpu.VMEM((n, MSG_ROWS, DH), BF16),
            pltpu.VMEM((n * HEAD_ROWS if n <= 64 else ROWS, n * owned), F32),
            pltpu.VMEM((n * owned, DH), F32),
            pltpu.VMEM((n * owned, DH), F32),
            pltpu.VMEM((n, owned, DH), BF16),
            pltpu.VMEM((n + HK, owned, DH), BF16),
            pltpu.VMEM((n, MSG_ROWS, DH), BF16),
            pltpu.VMEM((n + HK, MSG_ROWS, DH), BF16),
            pltpu.VMEM((TEAM, tok, span), BF16),
            pltpu.VMEM((TEAM, tok, span), BF16),
            pltpu.VMEM((span, TEAM * tok), BF16),
            pltpu.VMEM((tok, kv), BF16),
            pltpu.VMEM((TEAM, tok, kv), BF16),
            pltpu.VMEM((teams, width, kv), F32),
            pltpu.VMEM((teams, width, kv), BF16),
            pltpu.VMEM((teams, width, kv), BF16),
            pltpu.SemaphoreType.DMA((7,)),
            pltpu.SemaphoreType.DMA((4,)),
            pltpu.SemaphoreType.DMA((7,)),
            pltpu.SemaphoreType.DMA((7,)),
            pltpu.SemaphoreType.DMA((7,)),
            pltpu.SemaphoreType.DMA((7,)),
        ],
        compiler_params=pltpu.CompilerParams(
            collective_id=0, has_side_effects=True, vmem_limit_bytes=62 * 2**20
        ),
    )(hidden_in, queries, keys, values, grad_attn, send_rows, slot_docs)
    return pl.pallas_call(
        hand_over,
        out_shape=results,
        in_specs=[whole] * 4,
        out_specs=(whole,) * 4,
        scratch_shapes=[
            pltpu.SemaphoreType.DMA((4 * PARTS,)),
        ],
        compiler_params=pltpu.CompilerParams(vmem_limit_bytes=62 * 2**20),
    )(*outs)


def solution(mesh):
    placed = (
        P("dp", None),
        P("dp", None),
        P("dp", None),
        P("dp", None),
        P("dp", None),
        P(),
        P("dp", None),
    )
    return jax.shard_map(
        local,
        mesh=mesh,
        in_specs=placed,
        out_specs=(P("dp", None), P("dp", None), P("dp", None), P("dp", None)),
        check_vma=False,
    )
```

```python
import functools
import math

import jax
import jax.numpy as jnp
from jax import lax
from jax.experimental import pallas as pl
from jax.experimental.pallas import tpu as pltpu
from jax.sharding import PartitionSpec as P

HQ = 16
HK = 4
DH = 128
PER_KV = HQ // HK
ROWS = 8
HALO = 3
TEAM = 16
HALF = ROWS // 2
MESH = pl.DeviceIdType.MESH
F32 = jnp.float32
BF16 = jnp.bfloat16

HEAD_ROWS = PER_KV * ROWS
MSG_ROWS = HEAD_ROWS + 2 * ROWS


def dot(a, b, da, db):
    return lax.dot_general(a, b, (((da,), (db,)), ((), ())), preferred_element_type=F32)


def turn(x):
    return pltpu.roll(x, HALF, x.ndim - 2)


def low_line(x):
    return lax.broadcasted_iota(jnp.int32, x.shape, x.ndim - 2) < HALF


def halves_of(x, y):
    low = low_line(x)
    return jnp.where(low, x, turn(y)), jnp.where(low, turn(x), y)


def wait_bytes(ref, count, sem):
    view = ref.at[pl.ds(0, count)]
    pltpu.make_async_copy(view, view, sem).wait()


def kernel(
    n, width,
    hid_hbm, q_hbm, k_hbm, v_hbm, o_hbm, rows_hbm, docs_hbm,
    dq_hbm, dk_hbm, dv_hbm, dw_hbm,
    hid_ref, q_ref, k_ref, v_ref, o_ref, rows_ref, docs_ref, dq_ref, dk_ref, dw_ref,
    q32, o32, k32, v32, stage_s, came_s, stage_g, came_g, probs, k_rows, v_rows, acc_v, acc_k,
    back_v, home_v, back, home, hid_out, hid_in, hid_t, gv, gv_in, terms, term_out, term_in,
    loaded, stored, sent, got, near, near_got,
):
    me = lax.axis_index("dp")
    tok = q_ref.shape[0]
    groups = n // HK
    teams = n // TEAM
    member = lax.rem(me, TEAM)
    team = lax.div(me, TEAM)
    core = lax.rem(me, 2)
    spot = lax.rem(lax.div(me, 2), 4)
    side = lax.rem(lax.div(me, 8), 2)

    def place_in_team(a_core, a_side, a_spot):
        return a_core * 8 + a_side * 4 + a_spot

    my_place = place_in_team(core, side, spot)

    def device_at(a_core, a_side, a_spot):
        return team * TEAM + a_side * 8 + a_spot * 2 + a_core

    group = lax.div(me, HK)
    scale = 1.0 / math.sqrt(DH)
    keys = n * ROWS
    chunk = 16
    q_rows = chunk * HEAD_ROWS // 2

    loads = [
        pltpu.make_async_copy(src, dst, loaded.at[i])
        for i, (src, dst) in enumerate(
            (
                (q_hbm, q_ref),
                (k_hbm, k_ref),
                (docs_hbm, docs_ref),
                (o_hbm, o_ref),
                (v_hbm, v_ref),
                (hid_hbm, hid_ref),
                (rows_hbm, rows_ref),
            )
        )
    ]
    for load in loads:
        load.start()

    barrier = pltpu.get_barrier_semaphore()

    def greet(i, c):
        pl.semaphore_signal(
            barrier, inc=1, device_id=(lax.rem(me + i, n),), device_id_type=MESH
        )
        return c

    lax.fori_loop(1, n, greet, 0)

    k32[0:ROWS, :] = jnp.zeros((ROWS, k32.shape[1]), F32)
    v32[0:ROWS, :] = jnp.zeros((ROWS, v32.shape[1]), F32)
    for load in loads[:3]:
        load.wait()
    q32[...] = q_ref[...].astype(F32)
    k32[ROWS:, :] = k_ref[...].astype(F32)
    lane = lax.broadcasted_iota(jnp.int32, (2 * ROWS, DH), 1)
    line = lax.broadcasted_iota(jnp.int32, (2 * ROWS, DH), 0)
    doc_line = jnp.zeros((2 * ROWS, DH), F32)
    for j in range(docs_ref.shape[1]):
        doc_line = jnp.where(lane == j, (docs_ref[0, j] + 1).astype(F32), doc_line)

    def packer(dst, heads, tail, with_docs):
        def pack(g, c):
            at = pl.multiple_of(g * ROWS, ROWS)
            for h in range(HK):
                pairs = [
                    halves_of(
                        heads[pl.ds(at, ROWS), pl.ds((PER_KV * h + i) * DH, DH)],
                        heads[pl.ds(at, ROWS), pl.ds((PER_KV * h + i + 1) * DH, DH)],
                    )
                    for i in range(0, PER_KV, 2)
                ]
                parts = [pair[b] for b in range(2) for pair in pairs]
                part = tail[pl.ds(at, 2 * ROWS), pl.ds(h * DH, DH)]
                parts.append(jnp.where(line == 0, doc_line, part) if with_docs else part)
                dst[HK * g + h] = jnp.concatenate(parts, axis=0).astype(BF16)
            return c

        return pack

    def to_all(src, dst, index):
        def send(i, c):
            peer = lax.rem(me + i * 9, n)
            pltpu.make_async_remote_copy(
                src.at[peer], dst.at[me], sent.at[index], got.at[index],
                device_id=(peer,), device_id_type=MESH,
            ).start()
            return c

        lax.fori_loop(1, n, send, 0)

    lax.fori_loop(0, groups, packer(stage_s, q32, k32, True), 0)
    pl.semaphore_wait(barrier, n - 1)
    to_all(stage_s, came_s, 0)

    for load in loads[5:]:
        load.wait()
    span = hid_out.shape[2]
    for m in range(TEAM):
        if width % DH == 0:
            for p in range(teams):
                hid_out[m, :, p * width : (p + 1) * width] = hid_ref[
                    :, (p * TEAM + m) * width : (p * TEAM + m + 1) * width
                ]
        else:
            hid_out[m] = hid_ref[:, m * span : (m + 1) * span]
    for i in range(1, TEAM):
        other = lax.rem(member + i, TEAM)
        pltpu.make_async_remote_copy(
            hid_out.at[other], hid_in.at[my_place], sent.at[1], got.at[1],
            device_id=(team * TEAM + other,), device_id_type=MESH,
        ).start()
    hid_in[my_place] = hid_out[member]

    for load in loads[3:5]:
        load.wait()
    o32[...] = o_ref[...].astype(F32)
    v32[ROWS:, :] = v_ref[...].astype(F32)
    lax.fori_loop(0, groups, packer(stage_g, o32, v32, False), 0)
    to_all(stage_g, came_g, 6)

    came_s[me] = stage_s[me]
    came_g[me] = stage_g[me]
    acc_v[...] = jnp.zeros_like(acc_v)
    acc_k[...] = jnp.zeros_like(acc_k)
    home_v[n:, :, :] = jnp.zeros((HK, 2 * ROWS, DH), BF16)
    home[n:, :, :] = jnp.zeros((HK, MSG_ROWS, DH), BF16)

    wait_bytes(came_s, n - 1, got.at[0])

    doc_rows = came_s[:, HEAD_ROWS:, :][:, 0, :]
    pick = (
        lax.broadcasted_iota(jnp.int32, (8, DH), 0) == lax.broadcasted_iota(jnp.int32, (8, DH), 1)
    ).astype(F32).astype(BF16)
    doc_table = dot(pick, doc_rows, 1, 1)
    loc = lax.broadcasted_iota(jnp.int32, (2 * ROWS, n), 0) + (group - 1) * ROWS
    doc_sum = jnp.zeros((2 * ROWS, n), F32)
    for j in range(rows_ref.shape[0]):
        doc_sum += jnp.where(rows_ref[j : j + 1, :] == loc, doc_table[j : j + 1, :], 0.0)
    docs = jnp.sum(doc_sum, axis=1, keepdims=True)
    own_docs = docs[ROWS:]
    back_count = jnp.zeros((ROWS, 1), F32)
    for d in range(1, HALO + 1):
        back_count += jnp.where(docs[ROWS - d : 2 * ROWS - d] == own_docs, 1.0, 0.0)
    first = jnp.broadcast_to(
        (lax.broadcasted_iota(jnp.int32, (ROWS, 1), 0).astype(F32) - back_count) * n, (ROWS, DH)
    )
    firsts = [
        jnp.broadcast_to(
            part.astype(jnp.int32)[None, :, 0:1], (q_rows // ROWS, ROWS, 1)
        ).reshape(q_rows, 1)
        for part in halves_of(first, first)
    ]
    col = lax.broadcasted_iota(jnp.int32, (1, keys), 1)
    k_pos = (lax.rem(col, ROWS) - HALF) * n + lax.div(col, ROWS)
    row = lax.broadcasted_iota(jnp.int32, (q_rows, 1), 0)
    q_pos = lax.rem(row, HALF) * n + lax.div(row, HEAD_ROWS // 2)

    def spread(dst, src):
        both = src[:, HEAD_ROWS:, :].astype(F32)
        before, now = both[:, :ROWS], both[:, ROWS:]
        mixed = turn(jnp.where(low_line(now), now, before))
        dst[0] = mixed.reshape(keys, DH).astype(BF16)
        dst[1] = now.reshape(keys, DH).astype(BF16)

    def gathered(acc):
        early = turn(acc[0].reshape(n, ROWS, DH))
        late = acc[1].reshape(n, ROWS, DH)
        low = low_line(late)
        rows = [jnp.where(low, 0.0, early), jnp.where(low, early + late, late)]
        return jnp.concatenate(rows, axis=1).astype(BF16)

    def rows_of(ref, b, c):
        cut = slice(b * HEAD_ROWS // 2, (b + 1) * HEAD_ROWS // 2)
        return ref[pl.ds(c * chunk, chunk), cut, :].reshape(q_rows, DH)

    def prob_of(b, c):
        scores = dot(rows_of(came_s, b, c), k_rows[b], 1, 1)
        pos = k_pos + b * HALF * n
        allowed = (pos >= firsts[b]) & (pos <= q_pos + (c * chunk + b * HALF * n))
        scores = jnp.where(allowed, scores, -1000000000.0)
        top = jnp.max(scores, axis=1, keepdims=True)
        weights = jnp.exp2((scores - top) * (scale * math.log2(math.e)))
        return weights * (1.0 / jnp.sum(weights, axis=1, keepdims=True))

    kept = probs.shape[1] > q_rows

    def prob_rows(c):
        return pl.ds(pl.multiple_of(c * q_rows, q_rows), q_rows)

    def soft(c, carry):
        for b in range(2):
            probs[b, prob_rows(c), :] = prob_of(b, c)
        return carry

    spread(k_rows, came_s)
    if kept:
        lax.fori_loop(0, n // chunk, soft, 0)

    wait_bytes(came_g, n - 1, got.at[6])

    def value_grads(c, carry):
        for b in range(2):
            p = probs[b, prob_rows(c), :] if kept else prob_of(b, c)
            acc_v[b] += dot(p.astype(BF16), rows_of(came_g, b, c), 0, 0)
        return carry

    lax.fori_loop(0, n // chunk, value_grads, 0)
    back_v[...] = gathered(acc_v)
    to_all(back_v, home_v, 2)
    home_v[me] = back_v[me]
    spread(v_rows, came_g)

    def grads(c, carry):
        for b in range(2):
            p = probs[b, prob_rows(c), :] if kept else prob_of(b, c)
            dprob = dot(rows_of(came_g, b, c), v_rows[b], 1, 1)
            delta = jnp.sum(p * dprob, axis=1, keepdims=True)
            dscore = (p * (dprob - delta) * scale).astype(BF16)
            dq = dot(dscore, k_rows[b], 1, 0).astype(BF16)
            cut = slice(b * HEAD_ROWS // 2, (b + 1) * HEAD_ROWS // 2)
            back[pl.ds(c * chunk, chunk), cut, :] = dq.reshape(chunk, HEAD_ROWS // 2, DH)
            acc_k[b] += dot(dscore, rows_of(came_s, b, c), 0, 0)
        return carry

    lax.fori_loop(0, n // chunk, grads, 0)
    back[:, HEAD_ROWS:, :] = gathered(acc_k)

    wait_bytes(hid_in, TEAM - 1, got.at[1])
    tile = DH // min(tok, DH)
    for t in range(TEAM * tok // DH):
        if tile > 1:
            rows = hid_in[t * tile : (t + 1) * tile].reshape(DH, span)
        else:
            per = tok // DH
            rows = hid_in[t // per, (t % per) * DH : (t % per + 1) * DH, :]
        hid_t[:, t * DH : (t + 1) * DH] = rows.T

    def summed(ref, g, h, at):
        own = ref[HK * g + h, at : at + 2 * ROWS, :].astype(F32)
        after = ref[HK * g + HK + h, at : at + 2 * ROWS, :].astype(F32)
        return own[ROWS:] + after[:ROWS]

    wait_bytes(home_v, n - 1, got.at[2])

    def place_v(pair, c):
        at = pl.multiple_of(pair * 2 * ROWS, 2 * ROWS)
        for h in range(HK):
            both = [summed(home_v, 2 * pair + s, h, 0) for s in range(2)]
            gv[pl.ds(at, 2 * ROWS), pl.ds(h * DH, DH)] = jnp.concatenate(both, axis=0).astype(BF16)
        return c

    lax.fori_loop(0, groups // 2, place_v, 0)

    def pass_on(src, place, device, send_sem, recv_sem):
        pltpu.make_async_remote_copy(
            src, gv_in.at[place], send_sem, recv_sem,
            device_id=(device,), device_id_type=MESH,
        ).start()

    partner_place = place_in_team(core, 1 - side, spot)
    sibling = device_at(1 - core, side, spot)
    pass_on(gv, my_place, device_at(core, 1 - side, spot), near.at[0], near_got.at[0])
    for i in range(1, 4):
        there = device_at(core, side, lax.rem(spot + i, 4))
        pass_on(gv, my_place, there, near.at[i], near_got.at[i])
    pass_on(gv, my_place, sibling, sent.at[4], got.at[4])
    store_v = pltpu.make_async_copy(gv, dv_hbm, stored.at[0])
    store_v.start()
    to_all(back, home, 3)
    home[me] = back[me]
    gv_in[my_place] = gv[...]

    def landed(i):
        pltpu.make_async_copy(gv, gv, near_got.at[i]).wait()

    def across(place):
        pass_on(gv_in.at[place], place, sibling, sent.at[4], got.at[4])

    landed(0)
    for i in range(1, 4):
        there = device_at(core, side, lax.rem(spot + i, 4))
        pass_on(gv_in.at[partner_place], partner_place, there, near.at[3 + i], near_got.at[3 + i])
    across(partner_place)
    for i in range(1, 4):
        landed(i)
        across(place_in_team(core, side, lax.rem(spot + 4 - i, 4)))
    for i in range(1, 4):
        landed(3 + i)
        across(place_in_team(core, 1 - side, lax.rem(spot + 4 - i, 4)))

    grad_scale = 1.0 / math.sqrt(tok * n)
    half = TEAM // 2 * tok

    def half_term(p, which):
        cols = hid_t[
            pl.ds(pl.multiple_of(p * width, width), width),
            pl.ds(pl.multiple_of(which * half, half), half),
        ]
        rows = gv_in[pl.ds(which * (TEAM // 2), TEAM // 2)].reshape(half, gv.shape[1])
        return dot(cols, rows, 1, 0) * grad_scale

    for i in range(teams):
        other = lax.rem(team + i, teams)
        terms[i] = half_term(other, core)
    wait_bytes(gv_in, TEAM // 2, got.at[4])

    for i in range(1, teams):
        other = lax.rem(team + i, teams)
        term_out[other] = (terms[i] + half_term(other, 1 - core)).astype(BF16)
        pltpu.make_async_remote_copy(
            term_out.at[other], term_in.at[team], sent.at[5], got.at[5],
            device_id=(other * TEAM + member,), device_id_type=MESH,
        ).start()
    dw_ref[...] = terms[0] + half_term(team, 1 - core)

    wait_bytes(home, n - 1, got.at[3])

    def place(pair, c):
        at = pl.multiple_of(pair * 2 * ROWS, 2 * ROWS)
        for h in range(HK):
            both = [summed(home, 2 * pair + s, h, HEAD_ROWS) for s in range(2)]
            dk_ref[pl.ds(at, 2 * ROWS), pl.ds(h * DH, DH)] = jnp.concatenate(
                both, axis=0
            ).astype(BF16)
            lower = home[HK * 2 * pair + h, 0:HEAD_ROWS, :].astype(F32)
            upper = home[HK * (2 * pair + 1) + h, 0:HEAD_ROWS, :].astype(F32)
            for i in range(0, PER_KV, 2):
                a = slice(i * HALF, i * HALF + ROWS)
                b = slice((PER_KV + i) * HALF, (PER_KV + i) * HALF + ROWS)
                heads = zip(halves_of(lower[a], lower[b]), halves_of(upper[a], upper[b]))
                for s, head in enumerate(heads):
                    dq_ref[pl.ds(at, 2 * ROWS), pl.ds((PER_KV * h + i + s) * DH, DH)] = (
                        jnp.concatenate(head, axis=0).astype(BF16)
                    )
        return c

    lax.fori_loop(0, groups // 2, place, 0)
    store_q = pltpu.make_async_copy(dq_ref, dq_hbm, stored.at[1])
    store_k = pltpu.make_async_copy(dk_ref, dk_hbm, stored.at[2])
    store_q.start()
    store_k.start()

    wait_bytes(term_in, teams - 1, got.at[5])
    total = dw_ref[...]
    for i in range(1, teams):
        total += term_in[lax.rem(team + i, teams)].astype(F32)
    dw_ref[...] = total
    store_w = pltpu.make_async_copy(dw_ref, dw_hbm, stored.at[3])
    store_w.start()

    wait_bytes(stage_s, n - 1, sent.at[0])
    wait_bytes(stage_g, n - 1, sent.at[6])
    wait_bytes(hid_out, TEAM - 1, sent.at[1])
    wait_bytes(back_v, n - 1, sent.at[2])
    wait_bytes(back, n - 1, sent.at[3])
    wait_bytes(gv_in, TEAM // 2, sent.at[4])
    for i in range(7):
        pltpu.make_async_copy(gv, gv, near.at[i]).wait()
    wait_bytes(term_out, teams - 1, sent.at[5])
    store_v.wait()
    store_q.wait()
    store_k.wait()
    store_w.wait()


def hand_over(*refs):
    count = (len(refs) - 2) // 3
    srcs, dsts, held = refs[:count], refs[count : 2 * count], refs[2 * count : 3 * count]
    in_sem, out_sem = refs[3 * count :]
    ins = [pltpu.make_async_copy(srcs[i], held[i], in_sem.at[i]) for i in range(count)]
    outs = [pltpu.make_async_copy(held[i], dsts[i], out_sem.at[i]) for i in range(count)]
    for copy in ins:
        copy.start()
    for i in range(count):
        ins[i].wait()
        outs[i].start()
    for copy in outs:
        copy.wait()


def local(hidden_in, queries, keys, values, grad_attn, send_rows, slot_docs):
    n = lax.axis_size("dp")
    tok, model = hidden_in.shape
    width = model // n
    teams = n // TEAM
    span = model // TEAM
    kv = keys.shape[1]
    if width % DH:
        hidden_in = (
            hidden_in.reshape(tok, teams, TEAM, width).swapaxes(1, 2).reshape(tok, model)
        )
    whole = pl.BlockSpec(memory_space=pl.ANY)
    owned = 2 * ROWS
    results = (
        jax.ShapeDtypeStruct(queries.shape, BF16),
        jax.ShapeDtypeStruct(keys.shape, BF16),
        jax.ShapeDtypeStruct(values.shape, BF16),
        jax.ShapeDtypeStruct((width, kv), F32),
    )
    outs = pl.pallas_call(
        functools.partial(kernel, n, width),
        out_shape=results,
        in_specs=[whole] * 7,
        out_specs=(whole,) * 4,
        scratch_shapes=[
            pltpu.VMEM(hidden_in.shape, BF16),
            pltpu.VMEM(queries.shape, BF16),
            pltpu.VMEM(keys.shape, BF16),
            pltpu.VMEM(values.shape, BF16),
            pltpu.VMEM(grad_attn.shape, BF16),
            pltpu.VMEM(send_rows.shape, jnp.int32),
            pltpu.SMEM(slot_docs.shape, jnp.int32),
            pltpu.VMEM(queries.shape, BF16),
            pltpu.VMEM(keys.shape, BF16),
            pltpu.VMEM((width, kv), F32),
            pltpu.VMEM(queries.shape, F32),
            pltpu.VMEM(queries.shape, F32),
            pltpu.VMEM((tok + ROWS, kv), F32),
            pltpu.VMEM((tok + ROWS, kv), F32),
            pltpu.VMEM((n, MSG_ROWS, DH), BF16),
            pltpu.VMEM((n, MSG_ROWS, DH), BF16),
            pltpu.VMEM((n, MSG_ROWS, DH), BF16),
            pltpu.VMEM((n, MSG_ROWS, DH), BF16),
            pltpu.VMEM((2, n * HEAD_ROWS // 2 if n <= 64 else ROWS, n * ROWS), F32),
            pltpu.VMEM((2, n * ROWS, DH), BF16),
            pltpu.VMEM((2, n * ROWS, DH), BF16),
            pltpu.VMEM((2, n * ROWS, DH), F32),
            pltpu.VMEM((2, n * ROWS, DH), F32),
            pltpu.VMEM((n, owned, DH), BF16),
            pltpu.VMEM((n + HK, owned, DH), BF16),
            pltpu.VMEM((n, MSG_ROWS, DH), BF16),
            pltpu.VMEM((n + HK, MSG_ROWS, DH), BF16),
            pltpu.VMEM((TEAM, tok, span), BF16),
            pltpu.VMEM((TEAM, tok, span), BF16),
            pltpu.VMEM((span, TEAM * tok), BF16),
            pltpu.VMEM((tok, kv), BF16),
            pltpu.VMEM((TEAM, tok, kv), BF16),
            pltpu.VMEM((teams, width, kv), F32),
            pltpu.VMEM((teams, width, kv), BF16),
            pltpu.VMEM((teams, width, kv), BF16),
            pltpu.SemaphoreType.DMA((7,)),
            pltpu.SemaphoreType.DMA((4,)),
            pltpu.SemaphoreType.DMA((7,)),
            pltpu.SemaphoreType.DMA((7,)),
            pltpu.SemaphoreType.DMA((7,)),
            pltpu.SemaphoreType.DMA((7,)),
        ],
        compiler_params=pltpu.CompilerParams(
            collective_id=0, has_side_effects=True, vmem_limit_bytes=62 * 2**20
        ),
    )(hidden_in, queries, keys, values, grad_attn, send_rows, slot_docs)
    return pl.pallas_call(
        hand_over,
        out_shape=results,
        in_specs=[whole] * 4,
        out_specs=(whole,) * 4,
        scratch_shapes=[
            *(pltpu.VMEM(out.shape, out.dtype) for out in results),
            pltpu.SemaphoreType.DMA((4,)),
            pltpu.SemaphoreType.DMA((4,)),
        ],
        compiler_params=pltpu.CompilerParams(vmem_limit_bytes=62 * 2**20),
    )(*outs)


def solution(mesh):
    placed = (
        P("dp", None),
        P("dp", None),
        P("dp", None),
        P("dp", None),
        P("dp", None),
        P(),
        P("dp", None),
    )
    return jax.shard_map(
        local,
        mesh=mesh,
        in_specs=placed,
        out_specs=(P("dp", None), P("dp", None), P("dp", None), P("dp", None)),
        check_vma=False,
    )
```

```python
import functools
import math

import jax
import jax.numpy as jnp
from jax import lax
from jax.experimental import pallas as pl
from jax.experimental.pallas import tpu as pltpu
from jax.sharding import PartitionSpec as P

HQ = 16
HK = 4
DH = 128
PER_KV = HQ // HK
ROWS = 8
HALO = 3
TEAM = 16
HALF = ROWS // 2
MESH = pl.DeviceIdType.MESH
F32 = jnp.float32
BF16 = jnp.bfloat16

HEAD_ROWS = PER_KV * ROWS
MSG_ROWS = HEAD_ROWS + 2 * ROWS


def dot(a, b, da, db):
    return lax.dot_general(a, b, (((da,), (db,)), ((), ())), preferred_element_type=F32)


def turn(x):
    return pltpu.roll(x, HALF, x.ndim - 2)


def low_line(x):
    return lax.broadcasted_iota(jnp.int32, x.shape, x.ndim - 2) < HALF


def halves_of(x, y):
    low = low_line(x)
    return jnp.where(low, x, turn(y)), jnp.where(low, turn(x), y)


def wait_bytes(ref, count, sem):
    view = ref.at[pl.ds(0, count)]
    pltpu.make_async_copy(view, view, sem).wait()


def kernel(
    n, width,
    hid_hbm, q_hbm, k_hbm, v_hbm, o_hbm, rows_hbm, docs_hbm,
    dq_hbm, dk_hbm, dv_hbm, dw_hbm,
    hid_ref, q_ref, k_ref, v_ref, o_ref, rows_ref, docs_ref, dq_ref, dk_ref, dw_ref,
    q32, o32, k32, v32, stage_s, came_s, stage_o, came_o, stage_v, came_v, probs, k_rows, v_rows, acc_v, acc_k,
    back_v, home_v, back, home, hid_out, hid_in, hid_t, gv, gv_in, terms, term_out, term_in,
    loaded, stored, sent, got, near, near_got,
):
    me = lax.axis_index("dp")
    tok = q_ref.shape[0]
    groups = n // HK
    teams = n // TEAM
    member = lax.rem(me, TEAM)
    team = lax.div(me, TEAM)
    core = lax.rem(me, 2)
    spot = lax.rem(lax.div(me, 2), 4)
    side = lax.rem(lax.div(me, 8), 2)

    def place_in_team(a_core, a_side, a_spot):
        return a_core * 8 + a_side * 4 + a_spot

    my_place = place_in_team(core, side, spot)

    def device_at(a_core, a_side, a_spot):
        return team * TEAM + a_side * 8 + a_spot * 2 + a_core

    group = lax.div(me, HK)
    scale = 1.0 / math.sqrt(DH)
    keys = n * ROWS
    chunk = 16
    q_rows = chunk * HEAD_ROWS // 2

    loads = [
        pltpu.make_async_copy(src, dst, loaded.at[i])
        for i, (src, dst) in enumerate(
            (
                (q_hbm, q_ref),
                (k_hbm, k_ref),
                (docs_hbm, docs_ref),
                (o_hbm, o_ref),
                (v_hbm, v_ref),
                (hid_hbm, hid_ref),
                (rows_hbm, rows_ref),
            )
        )
    ]
    for load in loads:
        load.start()

    barrier = pltpu.get_barrier_semaphore()

    def greet(i, c):
        pl.semaphore_signal(
            barrier, inc=1, device_id=(lax.rem(me + i, n),), device_id_type=MESH
        )
        return c

    lax.fori_loop(1, n, greet, 0)

    k32[0:ROWS, :] = jnp.zeros((ROWS, k32.shape[1]), F32)
    v32[0:ROWS, :] = jnp.zeros((ROWS, v32.shape[1]), F32)
    for load in loads[:3]:
        load.wait()
    q32[...] = q_ref[...].astype(F32)
    k32[ROWS:, :] = k_ref[...].astype(F32)
    lane = lax.broadcasted_iota(jnp.int32, (2 * ROWS, DH), 1)
    line = lax.broadcasted_iota(jnp.int32, (2 * ROWS, DH), 0)
    doc_line = jnp.zeros((2 * ROWS, DH), F32)
    for j in range(docs_ref.shape[1]):
        doc_line = jnp.where(lane == j, (docs_ref[0, j] + 1).astype(F32), doc_line)

    def packer(dst, heads, tail):
        def pack(g, c):
            at = pl.multiple_of(g * ROWS, ROWS)
            for h in range(HK):
                pairs = [
                    halves_of(
                        heads[pl.ds(at, ROWS), pl.ds((PER_KV * h + i) * DH, DH)],
                        heads[pl.ds(at, ROWS), pl.ds((PER_KV * h + i + 1) * DH, DH)],
                    )
                    for i in range(0, PER_KV, 2)
                ]
                parts = [pair[b] for b in range(2) for pair in pairs]
                if tail is not None:
                    part = tail[pl.ds(at, 2 * ROWS), pl.ds(h * DH, DH)]
                    parts.append(jnp.where(line == 0, doc_line, part))
                dst[HK * g + h] = jnp.concatenate(parts, axis=0).astype(BF16)
            return c

        return pack

    def to_all(src, dst, index, begin=1, end=n):
        def send(i, c):
            peer = lax.rem(me + i * 9, n)
            pltpu.make_async_remote_copy(
                src.at[peer], dst.at[me], sent.at[index], got.at[index],
                device_id=(peer,), device_id_type=MESH,
            ).start()
            return c

        lax.fori_loop(begin, end, send, 0)

    lax.fori_loop(0, groups, packer(stage_s, q32, k32), 0)
    pl.semaphore_wait(barrier, n - 1)
    to_all(stage_s, came_s, 0)

    loads[3].wait()
    o32[...] = o_ref[...].astype(F32)
    lax.fori_loop(0, groups, packer(stage_o, o32, None), 0)
    to_all(stage_o, came_o, 6)

    loads[4].wait()
    v32[ROWS:, :] = v_ref[...].astype(F32)

    def pack_v(g, c):
        at = pl.multiple_of(g * ROWS, ROWS)
        for h in range(HK):
            stage_v[HK * g + h] = v32[pl.ds(at, 2 * ROWS), pl.ds(h * DH, DH)].astype(BF16)
        return c

    lax.fori_loop(0, groups, pack_v, 0)
    to_all(stage_v, came_v, 7)

    for load in loads[5:]:
        load.wait()
    span = hid_out.shape[2]
    for m in range(TEAM):
        if width % DH == 0:
            for p in range(teams):
                hid_out[m, :, p * width : (p + 1) * width] = hid_ref[
                    :, (p * TEAM + m) * width : (p * TEAM + m + 1) * width
                ]
        else:
            hid_out[m] = hid_ref[:, m * span : (m + 1) * span]
    came_s[me] = stage_s[me]
    came_o[me] = stage_o[me]
    came_v[me] = stage_v[me]
    acc_v[...] = jnp.zeros_like(acc_v)
    acc_k[...] = jnp.zeros_like(acc_k)
    home_v[n:, :, :] = jnp.zeros((HK, 2 * ROWS, DH), BF16)
    home[n:, :, :] = jnp.zeros((HK, MSG_ROWS, DH), BF16)

    wait_bytes(came_s, n - 1, got.at[0])

    doc_rows = came_s[:, HEAD_ROWS:, :][:, 0, :]
    pick = (
        lax.broadcasted_iota(jnp.int32, (8, DH), 0) == lax.broadcasted_iota(jnp.int32, (8, DH), 1)
    ).astype(F32).astype(BF16)
    doc_table = dot(pick, doc_rows, 1, 1)
    loc = lax.broadcasted_iota(jnp.int32, (2 * ROWS, n), 0) + (group - 1) * ROWS
    doc_sum = jnp.zeros((2 * ROWS, n), F32)
    for j in range(rows_ref.shape[0]):
        doc_sum += jnp.where(rows_ref[j : j + 1, :] == loc, doc_table[j : j + 1, :], 0.0)
    docs = jnp.sum(doc_sum, axis=1, keepdims=True)
    own_docs = docs[ROWS:]
    back_count = jnp.zeros((ROWS, 1), F32)
    for d in range(1, HALO + 1):
        back_count += jnp.where(docs[ROWS - d : 2 * ROWS - d] == own_docs, 1.0, 0.0)
    first = jnp.broadcast_to(
        (lax.broadcasted_iota(jnp.int32, (ROWS, 1), 0).astype(F32) - back_count) * n, (ROWS, DH)
    )
    firsts = [
        jnp.broadcast_to(
            part.astype(jnp.int32)[None, :, 0:1], (q_rows // ROWS, ROWS, 1)
        ).reshape(q_rows, 1)
        for part in halves_of(first, first)
    ]
    col = lax.broadcasted_iota(jnp.int32, (1, keys), 1)
    k_pos = (lax.rem(col, ROWS) - HALF) * n + lax.div(col, ROWS)
    row = lax.broadcasted_iota(jnp.int32, (q_rows, 1), 0)
    q_pos = lax.rem(row, HALF) * n + lax.div(row, HEAD_ROWS // 2)

    def spread(dst, src):
        both = src.astype(F32)
        before, now = both[:, :ROWS], both[:, ROWS:]
        mixed = turn(jnp.where(low_line(now), now, before))
        dst[0] = mixed.reshape(keys, DH).astype(BF16)
        dst[1] = now.reshape(keys, DH).astype(BF16)

    def gathered(acc):
        early = turn(acc[0].reshape(n, ROWS, DH))
        late = acc[1].reshape(n, ROWS, DH)
        low = low_line(late)
        rows = [jnp.where(low, 0.0, early), jnp.where(low, early + late, late)]
        return jnp.concatenate(rows, axis=1).astype(BF16)

    def rows_of(ref, b, c):
        cut = slice(b * HEAD_ROWS // 2, (b + 1) * HEAD_ROWS // 2)
        return ref[pl.ds(c * chunk, chunk), cut, :].reshape(q_rows, DH)

    def prob_of(b, c):
        scores = dot(rows_of(came_s, b, c), k_rows[b], 1, 1)
        pos = k_pos + b * HALF * n
        allowed = (pos >= firsts[b]) & (pos <= q_pos + (c * chunk + b * HALF * n))
        scores = jnp.where(allowed, scores, -1000000000.0)
        top = jnp.max(scores, axis=1, keepdims=True)
        weights = jnp.exp2((scores - top) * (scale * math.log2(math.e)))
        return weights * (1.0 / jnp.sum(weights, axis=1, keepdims=True))

    kept = probs.shape[1] > q_rows

    def prob_rows(c):
        return pl.ds(pl.multiple_of(c * q_rows, q_rows), q_rows)

    def soft(c, carry):
        for b in range(2):
            probs[b, prob_rows(c), :] = prob_of(b, c)
        return carry

    spread(k_rows, came_s[:, HEAD_ROWS:, :])
    if kept:
        lax.fori_loop(0, n // chunk, soft, 0)

    wait_bytes(came_o, n - 1, got.at[6])

    def value_grads(c, carry):
        for b in range(2):
            p = probs[b, prob_rows(c), :] if kept else prob_of(b, c)
            acc_v[b] += dot(p.astype(BF16), rows_of(came_o, b, c), 0, 0)
        return carry

    lax.fori_loop(0, n // chunk, value_grads, 0)
    back_v[...] = gathered(acc_v)
    to_all(back_v, home_v, 2)
    home_v[me] = back_v[me]
    for i in range(1, TEAM):
        other = lax.rem(member + i, TEAM)
        pltpu.make_async_remote_copy(
            hid_out.at[other], hid_in.at[my_place], sent.at[1], got.at[1],
            device_id=(team * TEAM + other,), device_id_type=MESH,
        ).start()
    hid_in[my_place] = hid_out[member]

    wait_bytes(came_v, n - 1, got.at[7])
    spread(v_rows, came_v[...])

    def grads(c, carry):
        for b in range(2):
            p = probs[b, prob_rows(c), :] if kept else prob_of(b, c)
            dprob = dot(rows_of(came_o, b, c), v_rows[b], 1, 1)
            delta = jnp.sum(p * dprob, axis=1, keepdims=True)
            dscore = (p * (dprob - delta) * scale).astype(BF16)
            dq = dot(dscore, k_rows[b], 1, 0).astype(BF16)
            cut = slice(b * HEAD_ROWS // 2, (b + 1) * HEAD_ROWS // 2)
            back[pl.ds(c * chunk, chunk), cut, :] = dq.reshape(chunk, HEAD_ROWS // 2, DH)
            acc_k[b] += dot(dscore, rows_of(came_s, b, c), 0, 0)
        return carry

    lax.fori_loop(0, n // chunk, grads, 0)
    back[:, HEAD_ROWS:, :] = gathered(acc_k)
    to_all(back, home, 3, 1, n // 3)

    def summed(ref, g, h, at):
        own = ref[HK * g + h, at : at + 2 * ROWS, :].astype(F32)
        after = ref[HK * g + HK + h, at : at + 2 * ROWS, :].astype(F32)
        return own[ROWS:] + after[:ROWS]

    wait_bytes(home_v, n - 1, got.at[2])

    def place_v(pair, c):
        at = pl.multiple_of(pair * 2 * ROWS, 2 * ROWS)
        for h in range(HK):
            both = [summed(home_v, 2 * pair + s, h, 0) for s in range(2)]
            gv[pl.ds(at, 2 * ROWS), pl.ds(h * DH, DH)] = jnp.concatenate(both, axis=0).astype(BF16)
        return c

    lax.fori_loop(0, groups // 2, place_v, 0)

    def pass_on(src, place, device, send_sem, recv_sem):
        pltpu.make_async_remote_copy(
            src, gv_in.at[place], send_sem, recv_sem,
            device_id=(device,), device_id_type=MESH,
        ).start()

    partner_place = place_in_team(core, 1 - side, spot)
    sibling = device_at(1 - core, side, spot)
    pass_on(gv, my_place, device_at(core, 1 - side, spot), near.at[0], near_got.at[0])
    for i in range(1, 4):
        there = device_at(core, side, lax.rem(spot + i, 4))
        pass_on(gv, my_place, there, near.at[i], near_got.at[i])
    pass_on(gv, my_place, sibling, sent.at[4], got.at[4])
    store_v = pltpu.make_async_copy(gv, dv_hbm, stored.at[0])
    store_v.start()
    to_all(back, home, 3, n // 3, n)
    home[me] = back[me]
    gv_in[my_place] = gv[...]

    def landed(i):
        pltpu.make_async_copy(gv, gv, near_got.at[i]).wait()

    def across(place):
        pass_on(gv_in.at[place], place, sibling, sent.at[4], got.at[4])

    landed(0)
    for i in range(1, 4):
        there = device_at(core, side, lax.rem(spot + i, 4))
        pass_on(gv_in.at[partner_place], partner_place, there, near.at[3 + i], near_got.at[3 + i])
    across(partner_place)
    for i in range(1, 4):
        landed(i)
        across(place_in_team(core, side, lax.rem(spot + 4 - i, 4)))
    for i in range(1, 4):
        landed(3 + i)
        across(place_in_team(core, 1 - side, lax.rem(spot + 4 - i, 4)))

    wait_bytes(hid_in, TEAM - 1, got.at[1])
    tile = DH // min(tok, DH)
    for t in range(TEAM * tok // DH):
        if tile > 1:
            rows = hid_in[t * tile : (t + 1) * tile].reshape(DH, span)
        else:
            per = tok // DH
            rows = hid_in[t // per, (t % per) * DH : (t % per + 1) * DH, :]
        hid_t[:, t * DH : (t + 1) * DH] = rows.T

    grad_scale = 1.0 / math.sqrt(tok * n)
    half = TEAM // 2 * tok

    def half_term(p, which):
        cols = hid_t[
            pl.ds(pl.multiple_of(p * width, width), width),
            pl.ds(pl.multiple_of(which * half, half), half),
        ]
        rows = gv_in[pl.ds(which * (TEAM // 2), TEAM // 2)].reshape(half, gv.shape[1])
        return dot(cols, rows, 1, 0) * grad_scale

    for i in range(teams):
        other = lax.rem(team + i, teams)
        terms[i] = half_term(other, core)
    wait_bytes(gv_in, TEAM // 2, got.at[4])

    for i in range(1, teams):
        other = lax.rem(team + i, teams)
        term_out[other] = (terms[i] + half_term(other, 1 - core)).astype(BF16)
        pltpu.make_async_remote_copy(
            term_out.at[other], term_in.at[team], sent.at[5], got.at[5],
            device_id=(other * TEAM + member,), device_id_type=MESH,
        ).start()
    dw_ref[...] = terms[0] + half_term(team, 1 - core)

    wait_bytes(home, n - 1, got.at[3])

    def place(pair, c):
        at = pl.multiple_of(pair * 2 * ROWS, 2 * ROWS)
        for h in range(HK):
            both = [summed(home, 2 * pair + s, h, HEAD_ROWS) for s in range(2)]
            dk_ref[pl.ds(at, 2 * ROWS), pl.ds(h * DH, DH)] = jnp.concatenate(
                both, axis=0
            ).astype(BF16)
            lower = home[HK * 2 * pair + h, 0:HEAD_ROWS, :].astype(F32)
            upper = home[HK * (2 * pair + 1) + h, 0:HEAD_ROWS, :].astype(F32)
            for i in range(0, PER_KV, 2):
                a = slice(i * HALF, i * HALF + ROWS)
                b = slice((PER_KV + i) * HALF, (PER_KV + i) * HALF + ROWS)
                heads = zip(halves_of(lower[a], lower[b]), halves_of(upper[a], upper[b]))
                for s, head in enumerate(heads):
                    dq_ref[pl.ds(at, 2 * ROWS), pl.ds((PER_KV * h + i + s) * DH, DH)] = (
                        jnp.concatenate(head, axis=0).astype(BF16)
                    )
        return c

    lax.fori_loop(0, groups // 2, place, 0)
    store_q = pltpu.make_async_copy(dq_ref, dq_hbm, stored.at[1])
    store_k = pltpu.make_async_copy(dk_ref, dk_hbm, stored.at[2])
    store_q.start()
    store_k.start()

    wait_bytes(term_in, teams - 1, got.at[5])
    total = dw_ref[...]
    for i in range(1, teams):
        total += term_in[lax.rem(team + i, teams)].astype(F32)
    dw_ref[...] = total
    store_w = pltpu.make_async_copy(dw_ref, dw_hbm, stored.at[3])
    store_w.start()

    wait_bytes(stage_s, n - 1, sent.at[0])
    wait_bytes(stage_o, n - 1, sent.at[6])
    wait_bytes(stage_v, n - 1, sent.at[7])
    wait_bytes(hid_out, TEAM - 1, sent.at[1])
    wait_bytes(back_v, n - 1, sent.at[2])
    wait_bytes(back, n - 1, sent.at[3])
    wait_bytes(gv_in, TEAM // 2, sent.at[4])
    for i in range(7):
        pltpu.make_async_copy(gv, gv, near.at[i]).wait()
    wait_bytes(term_out, teams - 1, sent.at[5])
    store_v.wait()
    store_q.wait()
    store_k.wait()
    store_w.wait()


def hand_over(*refs):
    count = (len(refs) - 2) // 3
    srcs, dsts, held = refs[:count], refs[count : 2 * count], refs[2 * count : 3 * count]
    in_sem, out_sem = refs[3 * count :]
    ins = [pltpu.make_async_copy(srcs[i], held[i], in_sem.at[i]) for i in range(count)]
    outs = [pltpu.make_async_copy(held[i], dsts[i], out_sem.at[i]) for i in range(count)]
    for copy in ins:
        copy.start()
    for i in range(count):
        ins[i].wait()
        outs[i].start()
    for copy in outs:
        copy.wait()


def local(hidden_in, queries, keys, values, grad_attn, send_rows, slot_docs):
    n = lax.axis_size("dp")
    tok, model = hidden_in.shape
    width = model // n
    teams = n // TEAM
    span = model // TEAM
    kv = keys.shape[1]
    if width % DH:
        hidden_in = (
            hidden_in.reshape(tok, teams, TEAM, width).swapaxes(1, 2).reshape(tok, model)
        )
    whole = pl.BlockSpec(memory_space=pl.ANY)
    owned = 2 * ROWS
    results = (
        jax.ShapeDtypeStruct(queries.shape, BF16),
        jax.ShapeDtypeStruct(keys.shape, BF16),
        jax.ShapeDtypeStruct(values.shape, BF16),
        jax.ShapeDtypeStruct((width, kv), F32),
    )
    outs = pl.pallas_call(
        functools.partial(kernel, n, width),
        out_shape=results,
        in_specs=[whole] * 7,
        out_specs=(whole,) * 4,
        scratch_shapes=[
            pltpu.VMEM(hidden_in.shape, BF16),
            pltpu.VMEM(queries.shape, BF16),
            pltpu.VMEM(keys.shape, BF16),
            pltpu.VMEM(values.shape, BF16),
            pltpu.VMEM(grad_attn.shape, BF16),
            pltpu.VMEM(send_rows.shape, jnp.int32),
            pltpu.SMEM(slot_docs.shape, jnp.int32),
            pltpu.VMEM(queries.shape, BF16),
            pltpu.VMEM(keys.shape, BF16),
            pltpu.VMEM((width, kv), F32),
            pltpu.VMEM(queries.shape, F32),
            pltpu.VMEM(queries.shape, F32),
            pltpu.VMEM((tok + ROWS, kv), F32),
            pltpu.VMEM((tok + ROWS, kv), F32),
            pltpu.VMEM((n, MSG_ROWS, DH), BF16),
            pltpu.VMEM((n, MSG_ROWS, DH), BF16),
            pltpu.VMEM((n, HEAD_ROWS, DH), BF16),
            pltpu.VMEM((n, HEAD_ROWS, DH), BF16),
            pltpu.VMEM((n, owned, DH), BF16),
            pltpu.VMEM((n, owned, DH), BF16),
            pltpu.VMEM((2, n * HEAD_ROWS // 2 if n <= 64 else ROWS, n * ROWS), F32),
            pltpu.VMEM((2, n * ROWS, DH), BF16),
            pltpu.VMEM((2, n * ROWS, DH), BF16),
            pltpu.VMEM((2, n * ROWS, DH), F32),
            pltpu.VMEM((2, n * ROWS, DH), F32),
            pltpu.VMEM((n, owned, DH), BF16),
            pltpu.VMEM((n + HK, owned, DH), BF16),
            pltpu.VMEM((n, MSG_ROWS, DH), BF16),
            pltpu.VMEM((n + HK, MSG_ROWS, DH), BF16),
            pltpu.VMEM((TEAM, tok, span), BF16),
            pltpu.VMEM((TEAM, tok, span), BF16),
            pltpu.VMEM((span, TEAM * tok), BF16),
            pltpu.VMEM((tok, kv), BF16),
            pltpu.VMEM((TEAM, tok, kv), BF16),
            pltpu.VMEM((teams, width, kv), F32),
            pltpu.VMEM((teams, width, kv), BF16),
            pltpu.VMEM((teams, width, kv), BF16),
            pltpu.SemaphoreType.DMA((7,)),
            pltpu.SemaphoreType.DMA((4,)),
            pltpu.SemaphoreType.DMA((8,)),
            pltpu.SemaphoreType.DMA((8,)),
            pltpu.SemaphoreType.DMA((7,)),
            pltpu.SemaphoreType.DMA((7,)),
        ],
        compiler_params=pltpu.CompilerParams(
            collective_id=0, has_side_effects=True, vmem_limit_bytes=62 * 2**20
        ),
    )(hidden_in, queries, keys, values, grad_attn, send_rows, slot_docs)
    return pl.pallas_call(
        hand_over,
        out_shape=results,
        in_specs=[whole] * 4,
        out_specs=(whole,) * 4,
        scratch_shapes=[
            *(pltpu.VMEM(out.shape, out.dtype) for out in results),
            pltpu.SemaphoreType.DMA((4,)),
            pltpu.SemaphoreType.DMA((4,)),
        ],
        compiler_params=pltpu.CompilerParams(vmem_limit_bytes=62 * 2**20),
    )(*outs)


def solution(mesh):
    placed = (
        P("dp", None),
        P("dp", None),
        P("dp", None),
        P("dp", None),
        P("dp", None),
        P(),
        P("dp", None),
    )
    return jax.shard_map(
        local,
        mesh=mesh,
        in_specs=placed,
        out_specs=(P("dp", None), P("dp", None), P("dp", None), P("dp", None)),
        check_vma=False,
    )
```

```python
import functools
import math

import jax
import jax.numpy as jnp
from jax import lax
from jax.experimental import pallas as pl
from jax.experimental.pallas import tpu as pltpu
from jax.sharding import PartitionSpec as P

HQ = 16
HK = 4
DH = 128
PER_KV = HQ // HK
ROWS = 8
HALO = 3
TEAM = 16
HALF = ROWS // 2
MESH = pl.DeviceIdType.MESH
F32 = jnp.float32
BF16 = jnp.bfloat16

HEAD_ROWS = PER_KV * ROWS
MSG_ROWS = HEAD_ROWS + 2 * ROWS


def dot(a, b, da, db):
    return lax.dot_general(a, b, (((da,), (db,)), ((), ())), preferred_element_type=F32)


def turn(x):
    return pltpu.roll(x, HALF, x.ndim - 2)


def low_line(x):
    return lax.broadcasted_iota(jnp.int32, x.shape, x.ndim - 2) < HALF


def halves_of(x, y):
    low = low_line(x)
    return jnp.where(low, x, turn(y)), jnp.where(low, turn(x), y)


def wait_bytes(ref, count, sem):
    view = ref.at[pl.ds(0, count)]
    pltpu.make_async_copy(view, view, sem).wait()


def kernel(
    n, width,
    hid_hbm, q_hbm, k_hbm, v_hbm, o_hbm, rows_hbm, docs_hbm,
    dq_hbm, dk_hbm, dv_hbm, dw_hbm,
    hid_ref, q_ref, k_ref, v_ref, o_ref, rows_ref, docs_ref, dq_ref, dk_ref, dw_ref,
    q32, o32, k32, v32, stage_s, came_s, stage_o, came_o, stage_v, came_v, probs, probs_t, k_rows, v_rows, acc_v, acc_k,
    back_v, home_v, back, home, hid_out, hid_in, hid_t, gv, gv_in, terms, term_out, term_in,
    loaded, stored, sent, got, near, near_got,
):
    me = lax.axis_index("dp")
    tok = q_ref.shape[0]
    groups = n // HK
    teams = n // TEAM
    member = lax.rem(me, TEAM)
    team = lax.div(me, TEAM)
    core = lax.rem(me, 2)
    spot = lax.rem(lax.div(me, 2), 4)
    side = lax.rem(lax.div(me, 8), 2)

    def place_in_team(a_core, a_side, a_spot):
        return a_core * 8 + a_side * 4 + a_spot

    my_place = place_in_team(core, side, spot)

    def device_at(a_core, a_side, a_spot):
        return team * TEAM + a_side * 8 + a_spot * 2 + a_core

    group = lax.div(me, HK)
    scale = 1.0 / math.sqrt(DH)
    keys = n * ROWS
    chunk = 16
    q_rows = chunk * HEAD_ROWS // 2

    loads = [
        pltpu.make_async_copy(src, dst, loaded.at[i])
        for i, (src, dst) in enumerate(
            (
                (q_hbm, q_ref),
                (k_hbm, k_ref),
                (docs_hbm, docs_ref),
                (o_hbm, o_ref),
                (v_hbm, v_ref),
                (hid_hbm, hid_ref),
                (rows_hbm, rows_ref),
            )
        )
    ]
    for load in loads:
        load.start()

    barrier = pltpu.get_barrier_semaphore()

    def greet(i, c):
        pl.semaphore_signal(
            barrier, inc=1, device_id=(lax.rem(me + i, n),), device_id_type=MESH
        )
        return c

    lax.fori_loop(1, n, greet, 0)

    k32[0:ROWS, :] = jnp.zeros((ROWS, k32.shape[1]), F32)
    v32[0:ROWS, :] = jnp.zeros((ROWS, v32.shape[1]), F32)
    for load in loads[:3]:
        load.wait()
    q32[...] = q_ref[...].astype(F32)
    k32[ROWS:, :] = k_ref[...].astype(F32)
    lane = lax.broadcasted_iota(jnp.int32, (2 * ROWS, DH), 1)
    line = lax.broadcasted_iota(jnp.int32, (2 * ROWS, DH), 0)
    doc_line = jnp.zeros((2 * ROWS, DH), F32)
    for j in range(docs_ref.shape[1]):
        doc_line = jnp.where(lane == j, (docs_ref[0, j] + 1).astype(F32), doc_line)

    def packer(dst, heads, tail):
        def pack(g, c):
            at = pl.multiple_of(g * ROWS, ROWS)
            for h in range(HK):
                pairs = [
                    halves_of(
                        heads[pl.ds(at, ROWS), pl.ds((PER_KV * h + i) * DH, DH)],
                        heads[pl.ds(at, ROWS), pl.ds((PER_KV * h + i + 1) * DH, DH)],
                    )
                    for i in range(0, PER_KV, 2)
                ]
                parts = [pair[b] for b in range(2) for pair in pairs]
                if tail is not None:
                    part = tail[pl.ds(at, 2 * ROWS), pl.ds(h * DH, DH)]
                    parts.append(jnp.where(line == 0, doc_line, part))
                dst[HK * g + h] = jnp.concatenate(parts, axis=0).astype(BF16)
            return c

        return pack

    def to_all(src, dst, index, begin=1, end=n):
        def send(i, c):
            peer = lax.rem(me + i * 9, n)
            pltpu.make_async_remote_copy(
                src.at[peer], dst.at[me], sent.at[index], got.at[index],
                device_id=(peer,), device_id_type=MESH,
            ).start()
            return c

        lax.fori_loop(begin, end, send, 0)

    lax.fori_loop(0, groups, packer(stage_s, q32, k32), 0)
    pl.semaphore_wait(barrier, n - 1)
    to_all(stage_s, came_s, 0)

    loads[3].wait()
    o32[...] = o_ref[...].astype(F32)
    lax.fori_loop(0, groups, packer(stage_o, o32, None), 0)
    to_all(stage_o, came_o, 6)

    loads[4].wait()
    v32[ROWS:, :] = v_ref[...].astype(F32)

    def pack_v(g, c):
        at = pl.multiple_of(g * ROWS, ROWS)
        for h in range(HK):
            stage_v[HK * g + h] = v32[pl.ds(at, 2 * ROWS), pl.ds(h * DH, DH)].astype(BF16)
        return c

    lax.fori_loop(0, groups, pack_v, 0)
    to_all(stage_v, came_v, 7)

    for load in loads[5:]:
        load.wait()
    span = hid_out.shape[2]
    for m in range(TEAM):
        if width % DH == 0:
            for p in range(teams):
                hid_out[m, :, p * width : (p + 1) * width] = hid_ref[
                    :, (p * TEAM + m) * width : (p * TEAM + m + 1) * width
                ]
        else:
            hid_out[m] = hid_ref[:, m * span : (m + 1) * span]
    came_s[me] = stage_s[me]
    came_o[me] = stage_o[me]
    came_v[me] = stage_v[me]
    acc_k[...] = jnp.zeros_like(acc_k)
    home_v[n:, :, :] = jnp.zeros((HK, 2 * ROWS, DH), BF16)
    home[n:, :, :] = jnp.zeros((HK, MSG_ROWS, DH), BF16)

    wait_bytes(came_s, n - 1, got.at[0])

    doc_rows = came_s[:, HEAD_ROWS:, :][:, 0, :]
    pick = (
        lax.broadcasted_iota(jnp.int32, (8, DH), 0) == lax.broadcasted_iota(jnp.int32, (8, DH), 1)
    ).astype(F32).astype(BF16)
    doc_table = dot(pick, doc_rows, 1, 1)
    loc = lax.broadcasted_iota(jnp.int32, (2 * ROWS, n), 0) + (group - 1) * ROWS
    doc_sum = jnp.zeros((2 * ROWS, n), F32)
    for j in range(rows_ref.shape[0]):
        doc_sum += jnp.where(rows_ref[j : j + 1, :] == loc, doc_table[j : j + 1, :], 0.0)
    docs = jnp.sum(doc_sum, axis=1, keepdims=True)
    own_docs = docs[ROWS:]
    back_count = jnp.zeros((ROWS, 1), F32)
    for d in range(1, HALO + 1):
        back_count += jnp.where(docs[ROWS - d : 2 * ROWS - d] == own_docs, 1.0, 0.0)
    first = jnp.broadcast_to(
        (lax.broadcasted_iota(jnp.int32, (ROWS, 1), 0).astype(F32) - back_count) * n, (ROWS, DH)
    )
    firsts = [
        jnp.broadcast_to(
            part.astype(jnp.int32)[None, :, 0:1], (q_rows // ROWS, ROWS, 1)
        ).reshape(q_rows, 1)
        for part in halves_of(first, first)
    ]
    col = lax.broadcasted_iota(jnp.int32, (1, keys), 1)
    k_pos = (lax.rem(col, ROWS) - HALF) * n + lax.div(col, ROWS)
    row = lax.broadcasted_iota(jnp.int32, (q_rows, 1), 0)
    q_pos = lax.rem(row, HALF) * n + lax.div(row, HEAD_ROWS // 2)

    def spread(dst, src):
        both = src.astype(F32)
        before, now = both[:, :ROWS], both[:, ROWS:]
        mixed = turn(jnp.where(low_line(now), now, before))
        dst[0] = mixed.reshape(keys, DH).astype(BF16)
        dst[1] = now.reshape(keys, DH).astype(BF16)

    def gathered(acc):
        early = turn(acc[0].reshape(n, ROWS, DH))
        late = acc[1].reshape(n, ROWS, DH)
        low = low_line(late)
        rows = [jnp.where(low, 0.0, early), jnp.where(low, early + late, late)]
        return jnp.concatenate(rows, axis=1).astype(BF16)

    def rows_of(ref, b, c):
        cut = slice(b * HEAD_ROWS // 2, (b + 1) * HEAD_ROWS // 2)
        return ref[pl.ds(c * chunk, chunk), cut, :].reshape(q_rows, DH)

    def prob_of(b, c):
        scores = dot(rows_of(came_s, b, c), k_rows[b], 1, 1)
        pos = k_pos + b * HALF * n
        allowed = (pos >= firsts[b]) & (pos <= q_pos + (c * chunk + b * HALF * n))
        scores = jnp.where(allowed, scores, -1000000000.0)
        top = jnp.max(scores, axis=1, keepdims=True)
        weights = jnp.exp2((scores - top) * (scale * math.log2(math.e)))
        return weights * (1.0 / jnp.sum(weights, axis=1, keepdims=True))

    kept = probs.shape[1] > q_rows

    def prob_rows(c):
        return pl.ds(pl.multiple_of(c * q_rows, q_rows), q_rows)

    def soft(c, carry):
        for b in range(2):
            p = prob_of(b, c)
            if kept:
                probs[b, prob_rows(c), :] = p
            probs_t[b, :, prob_rows(c)] = p.astype(BF16).T
        return carry

    spread(k_rows, came_s[:, HEAD_ROWS:, :])
    lax.fori_loop(0, n // chunk, soft, 0)

    wait_bytes(came_o, n - 1, got.at[6])

    for b in range(2):
        cut = slice(b * HEAD_ROWS // 2, (b + 1) * HEAD_ROWS // 2)
        acc_v[b] = dot(probs_t[b], came_o[:, cut, :].reshape(n * HEAD_ROWS // 2, DH), 1, 0)
    back_v[...] = gathered(acc_v)
    to_all(back_v, home_v, 2)
    home_v[me] = back_v[me]
    for i in range(1, TEAM):
        other = lax.rem(member + i, TEAM)
        pltpu.make_async_remote_copy(
            hid_out.at[other], hid_in.at[my_place], sent.at[1], got.at[1],
            device_id=(team * TEAM + other,), device_id_type=MESH,
        ).start()
    hid_in[my_place] = hid_out[member]

    wait_bytes(came_v, n - 1, got.at[7])
    spread(v_rows, came_v[...])

    def grads(c, carry):
        for b in range(2):
            p = probs[b, prob_rows(c), :] if kept else prob_of(b, c)
            dprob = dot(rows_of(came_o, b, c), v_rows[b], 1, 1)
            delta = jnp.sum(p * dprob, axis=1, keepdims=True)
            dscore = (p * (dprob - delta) * scale).astype(BF16)
            dq = dot(dscore, k_rows[b], 1, 0).astype(BF16)
            cut = slice(b * HEAD_ROWS // 2, (b + 1) * HEAD_ROWS // 2)
            back[pl.ds(c * chunk, chunk), cut, :] = dq.reshape(chunk, HEAD_ROWS // 2, DH)
            acc_k[b] += dot(dscore, rows_of(came_s, b, c), 0, 0)
        return carry

    lax.fori_loop(0, n // chunk, grads, 0)
    back[:, HEAD_ROWS:, :] = gathered(acc_k)
    to_all(back, home, 3, 1, n // 4)

    def summed(ref, g, h, at):
        own = ref[HK * g + h, at : at + 2 * ROWS, :].astype(F32)
        after = ref[HK * g + HK + h, at : at + 2 * ROWS, :].astype(F32)
        return own[ROWS:] + after[:ROWS]

    wait_bytes(home_v, n - 1, got.at[2])

    def place_v(pair, c):
        at = pl.multiple_of(pair * 2 * ROWS, 2 * ROWS)
        for h in range(HK):
            both = [summed(home_v, 2 * pair + s, h, 0) for s in range(2)]
            gv[pl.ds(at, 2 * ROWS), pl.ds(h * DH, DH)] = jnp.concatenate(both, axis=0).astype(BF16)
        return c

    lax.fori_loop(0, groups // 2, place_v, 0)

    def pass_on(src, place, device, send_sem, recv_sem):
        pltpu.make_async_remote_copy(
            src, gv_in.at[place], send_sem, recv_sem,
            device_id=(device,), device_id_type=MESH,
        ).start()

    sibling = device_at(1 - core, side, spot)
    chip = side * 4 + spot
    order = (4, 1, 7, 3, 5, 2, 6)
    for j in order:
        there = lax.rem(chip + j, 8)
        device = device_at(core, lax.div(there, 4), lax.rem(there, 4))
        pass_on(gv, my_place, device, near.at[j - 1], near_got.at[j - 1])
    pass_on(gv, my_place, sibling, sent.at[4], got.at[4])
    store_v = pltpu.make_async_copy(gv, dv_hbm, stored.at[0])
    store_v.start()
    to_all(back, home, 3, n // 4, n)
    home[me] = back[me]
    gv_in[my_place] = gv[...]

    for j in order:
        pltpu.make_async_copy(gv, gv, near_got.at[j - 1]).wait()
        place = core * 8 + lax.rem(chip + 8 - j, 8)
        pass_on(gv_in.at[place], place, sibling, sent.at[4], got.at[4])

    wait_bytes(hid_in, TEAM - 1, got.at[1])
    tile = DH // min(tok, DH)
    for t in range(TEAM * tok // DH):
        if tile > 1:
            rows = hid_in[t * tile : (t + 1) * tile].reshape(DH, span)
        else:
            per = tok // DH
            rows = hid_in[t // per, (t % per) * DH : (t % per + 1) * DH, :]
        hid_t[:, t * DH : (t + 1) * DH] = rows.T

    grad_scale = 1.0 / math.sqrt(tok * n)
    half = TEAM // 2 * tok

    def half_term(p, which):
        cols = hid_t[
            pl.ds(pl.multiple_of(p * width, width), width),
            pl.ds(pl.multiple_of(which * half, half), half),
        ]
        rows = gv_in[pl.ds(which * (TEAM // 2), TEAM // 2)].reshape(half, gv.shape[1])
        return dot(cols, rows, 1, 0) * grad_scale

    for i in range(teams):
        other = lax.rem(team + i, teams)
        terms[i] = half_term(other, core)
    wait_bytes(gv_in, TEAM // 2, got.at[4])

    for i in range(1, teams):
        other = lax.rem(team + i, teams)
        term_out[other] = (terms[i] + half_term(other, 1 - core)).astype(BF16)
        pltpu.make_async_remote_copy(
            term_out.at[other], term_in.at[team], sent.at[5], got.at[5],
            device_id=(other * TEAM + member,), device_id_type=MESH,
        ).start()
    dw_ref[...] = terms[0] + half_term(team, 1 - core)

    wait_bytes(home, n - 1, got.at[3])

    def place(pair, c):
        at = pl.multiple_of(pair * 2 * ROWS, 2 * ROWS)
        for h in range(HK):
            both = [summed(home, 2 * pair + s, h, HEAD_ROWS) for s in range(2)]
            dk_ref[pl.ds(at, 2 * ROWS), pl.ds(h * DH, DH)] = jnp.concatenate(
                both, axis=0
            ).astype(BF16)
            lower = home[HK * 2 * pair + h, 0:HEAD_ROWS, :].astype(F32)
            upper = home[HK * (2 * pair + 1) + h, 0:HEAD_ROWS, :].astype(F32)
            for i in range(0, PER_KV, 2):
                a = slice(i * HALF, i * HALF + ROWS)
                b = slice((PER_KV + i) * HALF, (PER_KV + i) * HALF + ROWS)
                heads = zip(halves_of(lower[a], lower[b]), halves_of(upper[a], upper[b]))
                for s, head in enumerate(heads):
                    dq_ref[pl.ds(at, 2 * ROWS), pl.ds((PER_KV * h + i + s) * DH, DH)] = (
                        jnp.concatenate(head, axis=0).astype(BF16)
                    )
        return c

    lax.fori_loop(0, groups // 2, place, 0)
    store_q = pltpu.make_async_copy(dq_ref, dq_hbm, stored.at[1])
    store_k = pltpu.make_async_copy(dk_ref, dk_hbm, stored.at[2])
    store_q.start()
    store_k.start()

    wait_bytes(term_in, teams - 1, got.at[5])
    total = dw_ref[...]
    for i in range(1, teams):
        total += term_in[lax.rem(team + i, teams)].astype(F32)
    dw_ref[...] = total
    store_w = pltpu.make_async_copy(dw_ref, dw_hbm, stored.at[3])
    store_w.start()

    wait_bytes(stage_s, n - 1, sent.at[0])
    wait_bytes(stage_o, n - 1, sent.at[6])
    wait_bytes(stage_v, n - 1, sent.at[7])
    wait_bytes(hid_out, TEAM - 1, sent.at[1])
    wait_bytes(back_v, n - 1, sent.at[2])
    wait_bytes(back, n - 1, sent.at[3])
    wait_bytes(gv_in, TEAM // 2, sent.at[4])
    for i in range(7):
        pltpu.make_async_copy(gv, gv, near.at[i]).wait()
    wait_bytes(term_out, teams - 1, sent.at[5])
    store_v.wait()
    store_q.wait()
    store_k.wait()
    store_w.wait()


def hand_over(*refs):
    count = (len(refs) - 2) // 3
    srcs, dsts, held = refs[:count], refs[count : 2 * count], refs[2 * count : 3 * count]
    in_sem, out_sem = refs[3 * count :]
    ins = [pltpu.make_async_copy(srcs[i], held[i], in_sem.at[i]) for i in range(count)]
    outs = [pltpu.make_async_copy(held[i], dsts[i], out_sem.at[i]) for i in range(count)]
    for copy in ins:
        copy.start()
    for i in range(count):
        ins[i].wait()
        outs[i].start()
    for copy in outs:
        copy.wait()


def local(hidden_in, queries, keys, values, grad_attn, send_rows, slot_docs):
    n = lax.axis_size("dp")
    tok, model = hidden_in.shape
    width = model // n
    teams = n // TEAM
    span = model // TEAM
    kv = keys.shape[1]
    if width % DH:
        hidden_in = (
            hidden_in.reshape(tok, teams, TEAM, width).swapaxes(1, 2).reshape(tok, model)
        )
    whole = pl.BlockSpec(memory_space=pl.ANY)
    owned = 2 * ROWS
    results = (
        jax.ShapeDtypeStruct(queries.shape, BF16),
        jax.ShapeDtypeStruct(keys.shape, BF16),
        jax.ShapeDtypeStruct(values.shape, BF16),
        jax.ShapeDtypeStruct((width, kv), F32),
    )
    outs = pl.pallas_call(
        functools.partial(kernel, n, width),
        out_shape=results,
        in_specs=[whole] * 7,
        out_specs=(whole,) * 4,
        scratch_shapes=[
            pltpu.VMEM(hidden_in.shape, BF16),
            pltpu.VMEM(queries.shape, BF16),
            pltpu.VMEM(keys.shape, BF16),
            pltpu.VMEM(values.shape, BF16),
            pltpu.VMEM(grad_attn.shape, BF16),
            pltpu.VMEM(send_rows.shape, jnp.int32),
            pltpu.SMEM(slot_docs.shape, jnp.int32),
            pltpu.VMEM(queries.shape, BF16),
            pltpu.VMEM(keys.shape, BF16),
            pltpu.VMEM((width, kv), F32),
            pltpu.VMEM(queries.shape, F32),
            pltpu.VMEM(queries.shape, F32),
            pltpu.VMEM((tok + ROWS, kv), F32),
            pltpu.VMEM((tok + ROWS, kv), F32),
            pltpu.VMEM((n, MSG_ROWS, DH), BF16),
            pltpu.VMEM((n, MSG_ROWS, DH), BF16),
            pltpu.VMEM((n, HEAD_ROWS, DH), BF16),
            pltpu.VMEM((n, HEAD_ROWS, DH), BF16),
            pltpu.VMEM((n, owned, DH), BF16),
            pltpu.VMEM((n, owned, DH), BF16),
            pltpu.VMEM((2, n * HEAD_ROWS // 2 if n <= 64 else ROWS, n * ROWS), F32),
            pltpu.VMEM((2, n * ROWS, n * HEAD_ROWS // 2), BF16),
            pltpu.VMEM((2, n * ROWS, DH), BF16),
            pltpu.VMEM((2, n * ROWS, DH), BF16),
            pltpu.VMEM((2, n * ROWS, DH), F32),
            pltpu.VMEM((2, n * ROWS, DH), F32),
            pltpu.VMEM((n, owned, DH), BF16),
            pltpu.VMEM((n + HK, owned, DH), BF16),
            pltpu.VMEM((n, MSG_ROWS, DH), BF16),
            pltpu.VMEM((n + HK, MSG_ROWS, DH), BF16),
            pltpu.VMEM((TEAM, tok, span), BF16),
            pltpu.VMEM((TEAM, tok, span), BF16),
            pltpu.VMEM((span, TEAM * tok), BF16),
            pltpu.VMEM((tok, kv), BF16),
            pltpu.VMEM((TEAM, tok, kv), BF16),
            pltpu.VMEM((teams, width, kv), F32),
            pltpu.VMEM((teams, width, kv), BF16),
            pltpu.VMEM((teams, width, kv), BF16),
            pltpu.SemaphoreType.DMA((7,)),
            pltpu.SemaphoreType.DMA((4,)),
            pltpu.SemaphoreType.DMA((8,)),
            pltpu.SemaphoreType.DMA((8,)),
            pltpu.SemaphoreType.DMA((7,)),
            pltpu.SemaphoreType.DMA((7,)),
        ],
        compiler_params=pltpu.CompilerParams(
            collective_id=0, has_side_effects=True, vmem_limit_bytes=62 * 2**20
        ),
    )(hidden_in, queries, keys, values, grad_attn, send_rows, slot_docs)
    return pl.pallas_call(
        hand_over,
        out_shape=results,
        in_specs=[whole] * 4,
        out_specs=(whole,) * 4,
        scratch_shapes=[
            *(pltpu.VMEM(out.shape, out.dtype) for out in results),
            pltpu.SemaphoreType.DMA((4,)),
            pltpu.SemaphoreType.DMA((4,)),
        ],
        compiler_params=pltpu.CompilerParams(vmem_limit_bytes=62 * 2**20),
    )(*outs)


def solution(mesh):
    placed = (
        P("dp", None),
        P("dp", None),
        P("dp", None),
        P("dp", None),
        P("dp", None),
        P(),
        P("dp", None),
    )
    return jax.shard_map(
        local,
        mesh=mesh,
        in_specs=placed,
        out_specs=(P("dp", None), P("dp", None), P("dp", None), P("dp", None)),
        check_vma=False,
    )
```

```python
import functools
import math

import jax
import jax.numpy as jnp
from jax import lax
from jax.experimental import pallas as pl
from jax.experimental.pallas import tpu as pltpu
from jax.sharding import PartitionSpec as P

HQ = 16
HK = 4
DH = 128
PER_KV = HQ // HK
ROWS = 8
HALO = 3
TEAM = 16
HALF = ROWS // 2
MESH = pl.DeviceIdType.MESH
F32 = jnp.float32
BF16 = jnp.bfloat16

HEAD_ROWS = PER_KV * ROWS
MSG_ROWS = HEAD_ROWS + 2 * ROWS


def dot(a, b, da, db):
    return lax.dot_general(a, b, (((da,), (db,)), ((), ())), preferred_element_type=F32)


def turn(x):
    return pltpu.roll(x, HALF, x.ndim - 2)


def low_line(x):
    return lax.broadcasted_iota(jnp.int32, x.shape, x.ndim - 2) < HALF


def halves_of(x, y):
    low = low_line(x)
    return jnp.where(low, x, turn(y)), jnp.where(low, turn(x), y)


def wait_bytes(ref, count, sem):
    view = ref.at[pl.ds(0, count)]
    pltpu.make_async_copy(view, view, sem).wait()


def kernel(
    n, width,
    hid_hbm, q_hbm, k_hbm, v_hbm, o_hbm, rows_hbm, docs_hbm,
    dq_hbm, dk_hbm, dv_hbm, dw_hbm,
    hid_ref, q_ref, k_ref, v_ref, o_ref, rows_ref, docs_ref, dq_ref, dk_ref, dw_ref,
    q32, o32, k32, v32, stage_s, came_s, stage_o, came_o, stage_v, came_v, probs, probs_t, k_rows, v_rows, acc_v, acc_k,
    back_v, home_v, back, home, hid_out, hid_in, hid_t, gv, gv_in, terms, term_out, term_in,
    loaded, stored, sent, got, near, near_got,
):
    me = lax.axis_index("dp")
    tok = q_ref.shape[0]
    groups = n // HK
    teams = n // TEAM
    member = lax.rem(me, TEAM)
    team = lax.div(me, TEAM)
    core = lax.rem(me, 2)
    spot = lax.rem(lax.div(me, 2), 4)
    side = lax.rem(lax.div(me, 8), 2)

    def place_in_team(a_core, a_side, a_spot):
        return a_core * 8 + a_side * 4 + a_spot

    my_place = place_in_team(core, side, spot)

    def device_at(a_core, a_side, a_spot):
        return team * TEAM + a_side * 8 + a_spot * 2 + a_core

    group = lax.div(me, HK)
    scale = 1.0 / math.sqrt(DH)
    keys = n * ROWS
    chunk = 16
    q_rows = chunk * HEAD_ROWS // 2

    loads = [
        pltpu.make_async_copy(src, dst, loaded.at[i])
        for i, (src, dst) in enumerate(
            (
                (q_hbm, q_ref),
                (k_hbm, k_ref),
                (docs_hbm, docs_ref),
                (o_hbm, o_ref),
                (v_hbm, v_ref),
                (hid_hbm, hid_ref),
                (rows_hbm, rows_ref),
            )
        )
    ]
    for load in loads:
        load.start()

    barrier = pltpu.get_barrier_semaphore()

    def greet(i, c):
        pl.semaphore_signal(
            barrier, inc=1, device_id=(lax.rem(me + i, n),), device_id_type=MESH
        )
        return c

    lax.fori_loop(1, n, greet, 0)

    k32[0:ROWS, :] = jnp.zeros((ROWS, k32.shape[1]), F32)
    v32[0:ROWS, :] = jnp.zeros((ROWS, v32.shape[1]), F32)
    for load in loads[:3]:
        load.wait()
    q32[...] = q_ref[...].astype(F32)
    k32[ROWS:, :] = k_ref[...].astype(F32)
    lane = lax.broadcasted_iota(jnp.int32, (2 * ROWS, DH), 1)
    line = lax.broadcasted_iota(jnp.int32, (2 * ROWS, DH), 0)
    doc_line = jnp.zeros((2 * ROWS, DH), F32)
    for j in range(docs_ref.shape[1]):
        doc_line = jnp.where(lane == j, (docs_ref[0, j] + 1).astype(F32), doc_line)

    def packer(dst, heads, tail):
        def pack(g, c):
            at = pl.multiple_of(g * ROWS, ROWS)
            for h in range(HK):
                pairs = [
                    halves_of(
                        heads[pl.ds(at, ROWS), pl.ds((PER_KV * h + i) * DH, DH)],
                        heads[pl.ds(at, ROWS), pl.ds((PER_KV * h + i + 1) * DH, DH)],
                    )
                    for i in range(0, PER_KV, 2)
                ]
                parts = [pair[b] for b in range(2) for pair in pairs]
                if tail is not None:
                    part = tail[pl.ds(at, 2 * ROWS), pl.ds(h * DH, DH)]
                    parts.append(jnp.where(line == 0, doc_line, part))
                dst[HK * g + h] = jnp.concatenate(parts, axis=0).astype(BF16)
            return c

        return pack

    def to_all(src, dst, index, begin=1, end=n):
        def send(i, c):
            peer = lax.rem(me + i * 9, n)
            pltpu.make_async_remote_copy(
                src.at[peer], dst.at[me], sent.at[index], got.at[index],
                device_id=(peer,), device_id_type=MESH,
            ).start()
            return c

        lax.fori_loop(begin, end, send, 0)

    lax.fori_loop(0, groups, packer(stage_s, q32, k32), 0)
    pl.semaphore_wait(barrier, n - 1)
    to_all(stage_s, came_s, 0)

    loads[3].wait()
    o32[...] = o_ref[...].astype(F32)
    lax.fori_loop(0, groups, packer(stage_o, o32, None), 0)
    to_all(stage_o, came_o, 6)

    loads[4].wait()
    v32[ROWS:, :] = v_ref[...].astype(F32)

    def pack_v(g, c):
        at = pl.multiple_of(g * ROWS, ROWS)
        for h in range(HK):
            stage_v[HK * g + h] = v32[pl.ds(at, 2 * ROWS), pl.ds(h * DH, DH)].astype(BF16)
        return c

    lax.fori_loop(0, groups, pack_v, 0)
    to_all(stage_v, came_v, 7)

    for load in loads[5:]:
        load.wait()
    span = hid_out.shape[2]
    for m in range(TEAM):
        if width % DH == 0:
            for p in range(teams):
                hid_out[m, :, p * width : (p + 1) * width] = hid_ref[
                    :, (p * TEAM + m) * width : (p * TEAM + m + 1) * width
                ]
        else:
            hid_out[m] = hid_ref[:, m * span : (m + 1) * span]
    for i in range(1, TEAM):
        other = lax.rem(member + i, TEAM)
        pltpu.make_async_remote_copy(
            hid_out.at[other], hid_in.at[my_place], sent.at[1], got.at[1],
            device_id=(team * TEAM + other,), device_id_type=MESH,
        ).start()
    hid_in[my_place] = hid_out[member]


    came_s[me] = stage_s[me]
    came_o[me] = stage_o[me]
    came_v[me] = stage_v[me]
    acc_k[...] = jnp.zeros_like(acc_k)
    home_v[n:, :, :] = jnp.zeros((HK, 2 * ROWS, DH), BF16)
    home[n:, :, :] = jnp.zeros((HK, MSG_ROWS, DH), BF16)

    wait_bytes(came_s, n - 1, got.at[0])

    doc_rows = came_s[:, HEAD_ROWS:, :][:, 0, :]
    pick = (
        lax.broadcasted_iota(jnp.int32, (8, DH), 0) == lax.broadcasted_iota(jnp.int32, (8, DH), 1)
    ).astype(F32).astype(BF16)
    doc_table = dot(pick, doc_rows, 1, 1)
    loc = lax.broadcasted_iota(jnp.int32, (2 * ROWS, n), 0) + (group - 1) * ROWS
    doc_sum = jnp.zeros((2 * ROWS, n), F32)
    for j in range(rows_ref.shape[0]):
        doc_sum += jnp.where(rows_ref[j : j + 1, :] == loc, doc_table[j : j + 1, :], 0.0)
    docs = jnp.sum(doc_sum, axis=1, keepdims=True)
    own_docs = docs[ROWS:]
    back_count = jnp.zeros((ROWS, 1), F32)
    for d in range(1, HALO + 1):
        back_count += jnp.where(docs[ROWS - d : 2 * ROWS - d] == own_docs, 1.0, 0.0)
    first = jnp.broadcast_to(
        (lax.broadcasted_iota(jnp.int32, (ROWS, 1), 0).astype(F32) - back_count) * n, (ROWS, DH)
    )
    firsts = [
        jnp.broadcast_to(
            part.astype(jnp.int32)[None, :, 0:1], (q_rows // ROWS, ROWS, 1)
        ).reshape(q_rows, 1)
        for part in halves_of(first, first)
    ]
    col = lax.broadcasted_iota(jnp.int32, (1, keys), 1)
    k_pos = (lax.rem(col, ROWS) - HALF) * n + lax.div(col, ROWS)
    row = lax.broadcasted_iota(jnp.int32, (q_rows, 1), 0)
    q_pos = lax.rem(row, HALF) * n + lax.div(row, HEAD_ROWS // 2)

    def spread(dst, src):
        both = src.astype(F32)
        before, now = both[:, :ROWS], both[:, ROWS:]
        mixed = turn(jnp.where(low_line(now), now, before))
        dst[0] = mixed.reshape(keys, DH).astype(BF16)
        dst[1] = now.reshape(keys, DH).astype(BF16)

    def gathered(acc):
        early = turn(acc[0].reshape(n, ROWS, DH))
        late = acc[1].reshape(n, ROWS, DH)
        low = low_line(late)
        rows = [jnp.where(low, 0.0, early), jnp.where(low, early + late, late)]
        return jnp.concatenate(rows, axis=1).astype(BF16)

    def rows_of(ref, b, c):
        cut = slice(b * HEAD_ROWS // 2, (b + 1) * HEAD_ROWS // 2)
        return ref[pl.ds(c * chunk, chunk), cut, :].reshape(q_rows, DH)

    def prob_of(b, c):
        scores = dot(rows_of(came_s, b, c), k_rows[b], 1, 1)
        pos = k_pos + b * HALF * n
        allowed = (pos >= firsts[b]) & (pos <= q_pos + (c * chunk + b * HALF * n))
        scores = jnp.where(allowed, scores, -1000000000.0)
        top = jnp.max(scores, axis=1, keepdims=True)
        weights = jnp.exp2((scores - top) * (scale * math.log2(math.e)))
        return weights * (1.0 / jnp.sum(weights, axis=1, keepdims=True))

    kept = probs.shape[1] > q_rows

    def prob_rows(c):
        return pl.ds(pl.multiple_of(c * q_rows, q_rows), q_rows)

    def soft(c, carry):
        for b in range(2):
            p = prob_of(b, c)
            if kept:
                probs[b, prob_rows(c), :] = p
            probs_t[b, :, prob_rows(c)] = p.astype(BF16).T
        return carry

    spread(k_rows, came_s[:, HEAD_ROWS:, :])
    lax.fori_loop(0, n // chunk, soft, 0)

    wait_bytes(came_o, n - 1, got.at[6])

    for b in range(2):
        cut = slice(b * HEAD_ROWS // 2, (b + 1) * HEAD_ROWS // 2)
        acc_v[b] = dot(probs_t[b], came_o[:, cut, :].reshape(n * HEAD_ROWS // 2, DH), 1, 0)
    back_v[...] = gathered(acc_v)
    to_all(back_v, home_v, 2)
    home_v[me] = back_v[me]
    wait_bytes(came_v, n - 1, got.at[7])
    spread(v_rows, came_v[...])

    def grads(c, carry):
        for b in range(2):
            p = probs[b, prob_rows(c), :] if kept else prob_of(b, c)
            dprob = dot(rows_of(came_o, b, c), v_rows[b], 1, 1)
            delta = jnp.sum(p * dprob, axis=1, keepdims=True)
            dscore = (p * (dprob - delta) * scale).astype(BF16)
            dq = dot(dscore, k_rows[b], 1, 0).astype(BF16)
            cut = slice(b * HEAD_ROWS // 2, (b + 1) * HEAD_ROWS // 2)
            back[pl.ds(c * chunk, chunk), cut, :] = dq.reshape(chunk, HEAD_ROWS // 2, DH)
            acc_k[b] += dot(dscore, rows_of(came_s, b, c), 0, 0)
        return carry

    lax.fori_loop(0, n // chunk, grads, 0)
    back[:, HEAD_ROWS:, :] = gathered(acc_k)
    to_all(back, home, 3, 1, n // 4)

    def summed(ref, g, h, at):
        own = ref[HK * g + h, at : at + 2 * ROWS, :].astype(F32)
        after = ref[HK * g + HK + h, at : at + 2 * ROWS, :].astype(F32)
        return own[ROWS:] + after[:ROWS]

    wait_bytes(home_v, n - 1, got.at[2])

    def place_v(pair, c):
        at = pl.multiple_of(pair * 2 * ROWS, 2 * ROWS)
        for h in range(HK):
            both = [summed(home_v, 2 * pair + s, h, 0) for s in range(2)]
            gv[pl.ds(at, 2 * ROWS), pl.ds(h * DH, DH)] = jnp.concatenate(both, axis=0).astype(BF16)
        return c

    lax.fori_loop(0, groups // 2, place_v, 0)

    def pass_on(src, place, device, send_sem, recv_sem):
        pltpu.make_async_remote_copy(
            src, gv_in.at[place], send_sem, recv_sem,
            device_id=(device,), device_id_type=MESH,
        ).start()

    sibling = device_at(1 - core, side, spot)
    chip = side * 4 + spot
    order = (4, 1, 7, 3, 5, 2, 6)
    for j in order:
        there = lax.rem(chip + j, 8)
        device = device_at(core, lax.div(there, 4), lax.rem(there, 4))
        pass_on(gv, my_place, device, near.at[j - 1], near_got.at[j - 1])
    pass_on(gv, my_place, sibling, sent.at[4], got.at[4])
    store_v = pltpu.make_async_copy(gv, dv_hbm, stored.at[0])
    store_v.start()
    to_all(back, home, 3, n // 4, n)
    home[me] = back[me]
    gv_in[my_place] = gv[...]

    for j in order:
        pltpu.make_async_copy(gv, gv, near_got.at[j - 1]).wait()
        place = core * 8 + lax.rem(chip + 8 - j, 8)
        pass_on(gv_in.at[place], place, sibling, sent.at[4], got.at[4])

    wait_bytes(hid_in, TEAM - 1, got.at[1])
    tile = DH // min(tok, DH)
    for t in range(TEAM * tok // DH):
        if tile > 1:
            rows = hid_in[t * tile : (t + 1) * tile].reshape(DH, span)
        else:
            per = tok // DH
            rows = hid_in[t // per, (t % per) * DH : (t % per + 1) * DH, :]
        hid_t[:, t * DH : (t + 1) * DH] = rows.T

    grad_scale = 1.0 / math.sqrt(tok * n)
    half = TEAM // 2 * tok

    def half_term(p, which):
        cols = hid_t[
            pl.ds(pl.multiple_of(p * width, width), width),
            pl.ds(pl.multiple_of(which * half, half), half),
        ]
        rows = gv_in[pl.ds(which * (TEAM // 2), TEAM // 2)].reshape(half, gv.shape[1])
        return dot(cols, rows, 1, 0) * grad_scale

    for i in range(teams):
        other = lax.rem(team + i, teams)
        terms[i] = half_term(other, core)
    wait_bytes(gv_in, TEAM // 2, got.at[4])

    for i in range(1, teams):
        other = lax.rem(team + i, teams)
        term_out[other] = (terms[i] + half_term(other, 1 - core)).astype(BF16)
        pltpu.make_async_remote_copy(
            term_out.at[other], term_in.at[team], sent.at[5], got.at[5],
            device_id=(other * TEAM + member,), device_id_type=MESH,
        ).start()
    dw_ref[...] = terms[0] + half_term(team, 1 - core)

    wait_bytes(home, n - 1, got.at[3])

    def place(pair, c):
        at = pl.multiple_of(pair * 2 * ROWS, 2 * ROWS)
        for h in range(HK):
            both = [summed(home, 2 * pair + s, h, HEAD_ROWS) for s in range(2)]
            dk_ref[pl.ds(at, 2 * ROWS), pl.ds(h * DH, DH)] = jnp.concatenate(
                both, axis=0
            ).astype(BF16)
            lower = home[HK * 2 * pair + h, 0:HEAD_ROWS, :].astype(F32)
            upper = home[HK * (2 * pair + 1) + h, 0:HEAD_ROWS, :].astype(F32)
            for i in range(0, PER_KV, 2):
                a = slice(i * HALF, i * HALF + ROWS)
                b = slice((PER_KV + i) * HALF, (PER_KV + i) * HALF + ROWS)
                heads = zip(halves_of(lower[a], lower[b]), halves_of(upper[a], upper[b]))
                for s, head in enumerate(heads):
                    dq_ref[pl.ds(at, 2 * ROWS), pl.ds((PER_KV * h + i + s) * DH, DH)] = (
                        jnp.concatenate(head, axis=0).astype(BF16)
                    )
        return c

    lax.fori_loop(0, groups // 2, place, 0)
    store_q = pltpu.make_async_copy(dq_ref, dq_hbm, stored.at[1])
    store_k = pltpu.make_async_copy(dk_ref, dk_hbm, stored.at[2])
    store_q.start()
    store_k.start()

    wait_bytes(term_in, teams - 1, got.at[5])
    total = dw_ref[...]
    for i in range(1, teams):
        total += term_in[lax.rem(team + i, teams)].astype(F32)
    dw_ref[...] = total
    store_w = pltpu.make_async_copy(dw_ref, dw_hbm, stored.at[3])
    store_w.start()

    wait_bytes(stage_s, n - 1, sent.at[0])
    wait_bytes(stage_o, n - 1, sent.at[6])
    wait_bytes(stage_v, n - 1, sent.at[7])
    wait_bytes(hid_out, TEAM - 1, sent.at[1])
    wait_bytes(back_v, n - 1, sent.at[2])
    wait_bytes(back, n - 1, sent.at[3])
    wait_bytes(gv_in, TEAM // 2, sent.at[4])
    for i in range(7):
        pltpu.make_async_copy(gv, gv, near.at[i]).wait()
    wait_bytes(term_out, teams - 1, sent.at[5])
    store_v.wait()
    store_q.wait()
    store_k.wait()
    store_w.wait()


def hand_over(*refs):
    count = (len(refs) - 2) // 3
    srcs, dsts, held = refs[:count], refs[count : 2 * count], refs[2 * count : 3 * count]
    in_sem, out_sem = refs[3 * count :]
    ins = [pltpu.make_async_copy(srcs[i], held[i], in_sem.at[i]) for i in range(count)]
    outs = [pltpu.make_async_copy(held[i], dsts[i], out_sem.at[i]) for i in range(count)]
    for copy in ins:
        copy.start()
    for i in range(count):
        ins[i].wait()
        outs[i].start()
    for copy in outs:
        copy.wait()


def local(hidden_in, queries, keys, values, grad_attn, send_rows, slot_docs):
    n = lax.axis_size("dp")
    tok, model = hidden_in.shape
    width = model // n
    teams = n // TEAM
    span = model // TEAM
    kv = keys.shape[1]
    if width % DH:
        hidden_in = (
            hidden_in.reshape(tok, teams, TEAM, width).swapaxes(1, 2).reshape(tok, model)
        )
    whole = pl.BlockSpec(memory_space=pl.ANY)
    owned = 2 * ROWS
    results = (
        jax.ShapeDtypeStruct(queries.shape, BF16),
        jax.ShapeDtypeStruct(keys.shape, BF16),
        jax.ShapeDtypeStruct(values.shape, BF16),
        jax.ShapeDtypeStruct((width, kv), F32),
    )
    outs = pl.pallas_call(
        functools.partial(kernel, n, width),
        out_shape=results,
        in_specs=[whole] * 7,
        out_specs=(whole,) * 4,
        scratch_shapes=[
            pltpu.VMEM(hidden_in.shape, BF16),
            pltpu.VMEM(queries.shape, BF16),
            pltpu.VMEM(keys.shape, BF16),
            pltpu.VMEM(values.shape, BF16),
            pltpu.VMEM(grad_attn.shape, BF16),
            pltpu.VMEM(send_rows.shape, jnp.int32),
            pltpu.SMEM(slot_docs.shape, jnp.int32),
            pltpu.VMEM(queries.shape, BF16),
            pltpu.VMEM(keys.shape, BF16),
            pltpu.VMEM((width, kv), F32),
            pltpu.VMEM(queries.shape, F32),
            pltpu.VMEM(queries.shape, F32),
            pltpu.VMEM((tok + ROWS, kv), F32),
            pltpu.VMEM((tok + ROWS, kv), F32),
            pltpu.VMEM((n, MSG_ROWS, DH), BF16),
            pltpu.VMEM((n, MSG_ROWS, DH), BF16),
            pltpu.VMEM((n, HEAD_ROWS, DH), BF16),
            pltpu.VMEM((n, HEAD_ROWS, DH), BF16),
            pltpu.VMEM((n, owned, DH), BF16),
            pltpu.VMEM((n, owned, DH), BF16),
            pltpu.VMEM((2, n * HEAD_ROWS // 2 if n <= 64 else ROWS, n * ROWS), F32),
            pltpu.VMEM((2, n * ROWS, n * HEAD_ROWS // 2), BF16),
            pltpu.VMEM((2, n * ROWS, DH), BF16),
            pltpu.VMEM((2, n * ROWS, DH), BF16),
            pltpu.VMEM((2, n * ROWS, DH), F32),
            pltpu.VMEM((2, n * ROWS, DH), F32),
            pltpu.VMEM((n, owned, DH), BF16),
            pltpu.VMEM((n + HK, owned, DH), BF16),
            pltpu.VMEM((n, MSG_ROWS, DH), BF16),
            pltpu.VMEM((n + HK, MSG_ROWS, DH), BF16),
            pltpu.VMEM((TEAM, tok, span), BF16),
            pltpu.VMEM((TEAM, tok, span), BF16),
            pltpu.VMEM((span, TEAM * tok), BF16),
            pltpu.VMEM((tok, kv), BF16),
            pltpu.VMEM((TEAM, tok, kv), BF16),
            pltpu.VMEM((teams, width, kv), F32),
            pltpu.VMEM((teams, width, kv), BF16),
            pltpu.VMEM((teams, width, kv), BF16),
            pltpu.SemaphoreType.DMA((7,)),
            pltpu.SemaphoreType.DMA((4,)),
            pltpu.SemaphoreType.DMA((8,)),
            pltpu.SemaphoreType.DMA((8,)),
            pltpu.SemaphoreType.DMA((7,)),
            pltpu.SemaphoreType.DMA((7,)),
        ],
        compiler_params=pltpu.CompilerParams(
            collective_id=0, has_side_effects=True, vmem_limit_bytes=62 * 2**20
        ),
    )(hidden_in, queries, keys, values, grad_attn, send_rows, slot_docs)
    return pl.pallas_call(
        hand_over,
        out_shape=results,
        in_specs=[whole] * 4,
        out_specs=(whole,) * 4,
        scratch_shapes=[
            *(pltpu.VMEM(out.shape, out.dtype) for out in results),
            pltpu.SemaphoreType.DMA((4,)),
            pltpu.SemaphoreType.DMA((4,)),
        ],
        compiler_params=pltpu.CompilerParams(vmem_limit_bytes=62 * 2**20),
    )(*outs)


def solution(mesh):
    placed = (
        P("dp", None),
        P("dp", None),
        P("dp", None),
        P("dp", None),
        P("dp", None),
        P(),
        P("dp", None),
    )
    return jax.shard_map(
        local,
        mesh=mesh,
        in_specs=placed,
        out_specs=(P("dp", None), P("dp", None), P("dp", None), P("dp", None)),
        check_vma=False,
    )
```
